512 devices in a mesh: wide: 64 (over y, z_lo, x), narrow: 8 (over z_hi, core).
Axes of the slice: x: 4, y: 8, z: 8 (z_hi: 4, z_lo: 2; z = z_hi * 2 + z_lo), core: 2. Of those that a mesh axis runs over, the one named last changes fastest.
Arguments:
- pressure: float32 [128, 2048, 128], P('narrow', 'wide'), may hold values from -6 to 6
- saturation: float32 [128, 2048, 128], P('narrow', 'wide'), may hold values from 0.1 to 0.9
- source: float32 [128, 2048, 128], P('narrow', 'wide'), may hold values from -6 to 6
- permeability: float32 [3, 128, 2048, 128], P(None, 'narrow', 'wide'), may hold values from 0.1 to 10
- pore_volume: float32 [128, 2048, 128], P('narrow', 'wide'), may hold values from 0.5 to 2
- basis: bfloat16 [128, 2048, 4, 128], P('narrow', 'wide'), may hold values from 0 to 1
- support: int32 [128, 2048, 4], P('narrow', 'wide'), may hold values from 0 to 8, all different within a row
- coarse_matrix: float32 [9, 128, 2048], P(None, 'narrow', 'wide'), may hold values from -44.8 to 768, as said below
Outputs:
- new_pressure: float32 [128, 2048, 128], P('narrow', 'wide')
- new_saturation: float32 [128, 2048, 128], P('narrow', 'wide')
The draws below stay inside these ranges and needn't reach their ends.
Inputs may be any that keep to these rules, and one draw needn't show every extreme that they name: `support`: the 4 codes of one column are distinct. `coarse_matrix`: entries at codes other than 4 are negative; the entry at code 4 exceeds the sum of magnitudes of the other eight of its block.
All inputs are finite; a program needn't handle non-finite values.
Results may differ from the reference program's by a relative error of at most 0.0003.
Values sent between devices are 32-bit elements; how exact they have to be, the bound alone decides.
No kernel may reach another device: no remote copies, remote signals or barrier semaphores. Data moves between devices by JAX's collectives and lax.ppermute only.
A program may use at most 64 MiB of HBM per device.

```python
import math
import jax
import jax.numpy as jnp
from jax import lax

L = 128
K = 4
SWEEPS = 3
NX = 128
NY = 2048


def draw_coarse_matrix(key, part):
    first_key, second_key = jax.random.split(jax.random.fold_in(key, 17))
    offdiag = jax.random.uniform(first_key, (8, NX, NY), jnp.float32, 0.05, 0.3)
    extra = jnp.exp(jax.random.uniform(second_key, (NX, NY), jnp.float32, jnp.log(0.5), jnp.log(2.0)))
    middle = jnp.sum(offdiag, axis=0) + extra
    stencil = jnp.concatenate([-offdiag[:4], middle[None], -offdiag[4:]], axis=0)
    return (stencil * L).astype(jnp.float32)


def levels(rng, dims, cuts, smallest, top_value):
    factor_of = 1.0
    for dim, blocks in cuts:
        steps = jax.random.uniform(jax.random.fold_in(jax.random.fold_in(rng, 6), dim), (blocks,), jnp.float32, smallest / len(cuts), top_value / len(cuts))
        factor_of = factor_of * jnp.repeat(jnp.exp(steps), dims[dim] // blocks).reshape((-1,) + (1,) * (len(dims) - 1 - dim))
    return factor_of


def picks_of(own_key, rows, amount, top, lift):
    ranking = jax.random.permutation(jax.random.fold_in(own_key, 1), amount)
    favour = ranking
    for power in range(3):
        favour = favour * favour // amount
    favour = favour * lift // amount
    chance = jax.random.randint(jax.random.fold_in(own_key, 2), (rows, amount), 0, 4096) + favour
    sure = jax.random.permutation(jax.random.fold_in(own_key, 3), rows)[jnp.arange(amount) % rows]
    chance = jnp.where(jnp.arange(rows)[:, None] == sure[None, :], 1 << 14, chance)
    priority = chance * amount + jnp.arange(amount)
    return lax.top_k(priority.astype(jnp.int32), top)[1].astype(jnp.int32)


def scatter_about(own_key, extent, deviation, bound, shards=(), held_as=jnp.bfloat16):
    entries = deviation * jax.random.normal(own_key, extent, jnp.float32)
    if shards:
        entries = entries * levels(own_key, extent, shards, -0.22, 0.18)
    return jnp.clip(entries, -bound, bound).astype(held_as)


def setup_inputs(seed: int = 0) -> dict:
    seeds = jax.random.split(jax.random.key(seed), 9)
    return {
        "pressure": scatter_about(seeds[0], (NX, NY, L), 1.0, 6.0, ((0, 8), (1, 64)), jnp.float32),
        "saturation": jnp.clip(0.1 + 0.79999997 * jax.random.uniform(seeds[1], (NX, NY, L), jnp.float32) ** levels(seeds[1], (NX, NY, L), ((0, 8), (1, 64)), -0.2, 0.2), 0.1, 0.9),
        "source": scatter_about(seeds[2], (NX, NY, L), 1.0, 6.0, ((0, 8), (1, 64)), jnp.float32),
        "permeability": jnp.clip(jnp.exp(math.log(10.0) - 4.6051702 * jax.random.uniform(seeds[3], (3, NX, NY, L), jnp.float32) ** levels(seeds[3], (3, NX, NY, L), ((1, 8), (2, 64)), -0.2, 0.2)), 0.1, 10.0),
        "pore_volume": jnp.clip(jnp.exp(math.log(2.0) - 1.3862944 * jax.random.uniform(seeds[4], (NX, NY, L), jnp.float32) ** levels(seeds[4], (NX, NY, L), ((0, 8), (1, 64)), -0.2, 0.2)), 0.5, 2.0),
        "basis": jnp.clip(1.0 * jax.random.uniform(seeds[5], (NX, NY, K, L), jnp.float32) ** levels(seeds[5], (NX, NY, K, L), ((0, 8), (1, 64)), -0.2, 0.2), 0.0, 1.0).astype(jnp.bfloat16),
        "support": picks_of(seeds[6], NX * NY, 9, K, 0).reshape((NX, NY, K)),
        "coarse_matrix": draw_coarse_matrix(jax.random.fold_in(seeds[8], 71), 0),
    }


OFFSETS = [(o // 3 - 1, o % 3 - 1) for o in range(9)]
DIRECTIONS = [(1, 0, 0, 0), (-1, 0, 0, 0), (0, 1, 0, 1), (0, -1, 0, 1), (0, 0, 1, 2), (0, 0, -1, 2)]
OMEGA = 0.6667
DT = 0.01


def neighbour(padded, step_x, step_y, step_z, count_x, count_y):
    depth = padded.shape[2] - 2
    return padded[1 + step_x:1 + step_x + count_x, 1 + step_y:1 + step_y + count_y, 1 + step_z:1 + step_z + depth]


def face_fluxes(pres_pad, perm_pads, count_x, count_y):
    centre = neighbour(pres_pad, 0, 0, 0, count_x, count_y)
    result = []
    for step_x, step_y, step_z, comp in DIRECTIONS:
        k_here = neighbour(perm_pads[comp], 0, 0, 0, count_x, count_y)
        k_there = neighbour(perm_pads[comp], step_x, step_y, step_z, count_x, count_y)
        trans = 2.0 * k_here * k_there / (k_here + k_there)
        result.append(trans * (centre - neighbour(pres_pad, step_x, step_y, step_z, count_x, count_y)))
    return result


def fraction(sat):
    return sat * sat / (sat * sat + 0.5 * (1.0 - sat) * (1.0 - sat))


def outflow(fluxes, sat_pad, count_x, count_y):
    centre = neighbour(sat_pad, 0, 0, 0, count_x, count_y)
    total = jnp.zeros_like(centre)
    for flux, (step_x, step_y, step_z, comp) in zip(fluxes, DIRECTIONS):
        other = neighbour(sat_pad, step_x, step_y, step_z, count_x, count_y)
        upwind = jnp.where(flux > 0, centre, other)
        total = total + flux * fraction(upwind)
    return total


def restrict_pieces(basis, support, residual):
    pieces = []
    for k in range(basis.shape[2]):
        pieces.append(jnp.sum(basis[:, :, k, :].astype(jnp.float32) * residual, axis=-1))
    binned = []
    for o in range(9):
        acc = jnp.zeros(residual.shape[:2], jnp.float32)
        for k in range(basis.shape[2]):
            acc = acc + jnp.where(support[:, :, k] == o, pieces[k], 0.0)
        binned.append(acc)
    return jnp.stack(binned)


def collect_pieces(binned_pad, count_x, count_y):
    total = jnp.zeros((count_x, count_y), jnp.float32)
    for o, (dx, dy) in enumerate(OFFSETS):
        total = total + binned_pad[o, 1 - dx:1 - dx + count_x, 1 - dy:1 - dy + count_y]
    return total


def apply_coarse(coarse_matrix, coarse_pad, count_x, count_y):
    total = jnp.zeros((count_x, count_y), jnp.float32)
    for o, (dx, dy) in enumerate(OFFSETS):
        total = total + coarse_matrix[o] * coarse_pad[1 + dx:1 + dx + count_x, 1 + dy:1 + dy + count_y]
    return total


def prolong(basis, support, coarse_pad, count_x, count_y):
    moved = [coarse_pad[1 + dx:1 + dx + count_x, 1 + dy:1 + dy + count_y] for dx, dy in OFFSETS]
    total = jnp.zeros(basis.shape[:2] + basis.shape[3:], jnp.float32)
    for k in range(basis.shape[2]):
        picked = jnp.zeros((count_x, count_y), jnp.float32)
        for o in range(9):
            picked = picked + jnp.where(support[:, :, k] == o, moved[o], 0.0)
        total = total + basis[:, :, k, :].astype(jnp.float32) * picked[:, :, None]
    return total


def reference(pressure, saturation, source, permeability, pore_volume, basis, support, coarse_matrix):
    pres_pad = jnp.pad(pressure, 1)
    perm_pads = [jnp.pad(permeability[c], 1) for c in range(3)]
    fluxes = face_fluxes(pres_pad, perm_pads, NX, NY)
    residual = source - sum(fluxes)
    binned = restrict_pieces(basis, support, residual)
    coarse_residual = collect_pieces(jnp.pad(binned, ((0, 0), (1, 1), (1, 1))), NX, NY)
    diag = coarse_matrix[4]
    coarse = OMEGA * coarse_residual / diag
    for sweep in range(SWEEPS - 1):
        coarse = coarse + OMEGA * (coarse_residual - apply_coarse(coarse_matrix, jnp.pad(coarse, 1), NX, NY)) / diag
    new_pressure = pressure + prolong(basis, support, jnp.pad(coarse, 1), NX, NY)
    new_fluxes = face_fluxes(jnp.pad(new_pressure, 1), perm_pads, NX, NY)
    total = outflow(new_fluxes, jnp.pad(saturation, 1), NX, NY)
    new_saturation = saturation - DT * total / pore_volume
    return new_pressure, new_saturation
```

```python
import jax
import jax.numpy as jnp
from jax import lax
from jax.sharding import PartitionSpec as P

SWEEPS = 3
OFFSETS = [(o // 3 - 1, o % 3 - 1) for o in range(9)]
OMEGA = 0.6667
DT = 0.01
REACH = SWEEPS + 1
EDGE = REACH + 1


def trans_of(here, there):
    total = here + there
    return 2.0 * here * there / jnp.where(total > 0, total, 1.0)


def fraction(sat):
    return sat * sat / (sat * sat + 0.5 * (1.0 - sat) * (1.0 - sat))


def shifted(array, dim, step):
    pad = jnp.zeros_like(lax.slice_in_dim(array, 0, 1, axis=dim))
    n = array.shape[dim]
    if step > 0:
        return jnp.concatenate([lax.slice_in_dim(array, 1, n, axis=dim), pad], axis=dim)
    return jnp.concatenate([pad, lax.slice_in_dim(array, 0, n - 1, axis=dim)], axis=dim)


def scatter(basis, support, residual):
    rows, cols = residual.shape[:2]
    pieces = jnp.sum(basis * residual[:, :, None, :], axis=-1)
    total = jnp.zeros((rows + 2, cols + 2), jnp.float32)
    for o, (dx, dy) in enumerate(OFFSETS):
        binned = jnp.sum(jnp.where(support == o, pieces, 0.0), axis=-1)
        total = total + jnp.pad(binned, ((1 + dx, 1 - dx), (1 + dy, 1 - dy)))
    return total


def pack(arrays):
    flat = jnp.concatenate([a.reshape(-1) for a in arrays])
    rows = -(-flat.shape[0] // 1024) * 8
    return jnp.pad(flat, (0, rows * 128 - flat.shape[0])).reshape(rows, 128)


def unpack(packed, likes):
    flat, at, out = packed.reshape(-1), 0, []
    for a in likes:
        out.append(flat[at : at + a.size].reshape(a.shape))
        at += a.size
    return out


def matchings(n):
    even = [(i, i + 1) for i in range(0, n - 1, 2)]
    odd = [(i, i + 1) for i in range(1, n - 1, 2)]
    return [p + [(j, i) for i, j in p] for p in (even, odd)]


def exchange(axis, first, last, gather):
    n = lax.axis_size(axis)
    is_even = lax.axis_index(axis) % 2 == 0
    even, odd = matchings(n)
    odd_in = lax.ppermute(jnp.where(is_even, first, last), axis, odd)
    mine = jnp.where(is_even, last, first)
    if gather:
        both = lax.all_gather(mine, axis, axis_index_groups=[[i, i + 1] for i in range(0, n, 2)])
        even_in = jnp.where(is_even, both[1], both[0])
    else:
        even_in = lax.ppermute(mine, axis, even)
    return jnp.where(is_even, odd_in, even_in), jnp.where(is_even, even_in, odd_in)


def pick(coarse, support, row, col):
    rows, cols = support.shape[:2]
    total = jnp.zeros(support.shape, jnp.float32)
    for o, (dx, dy) in enumerate(OFFSETS):
        moved = coarse[row + dx : row + dx + rows, col + dy : col + dy + cols]
        total = total + jnp.where(support == o, moved[:, :, None], 0.0)
    return total


def corrected(pressure, basis, support, coarse, row, col):
    return pressure + jnp.sum(basis * pick(coarse, support, row, col)[..., None], axis=2)


def on_device(pressure, saturation, source, perm, pore_volume, basis, support, matrix):
    nx, ny, _ = pressure.shape
    basis = basis.astype(jnp.float32)
    support = support.astype(jnp.float32)
    kx, ky, kz = perm[0], perm[1], perm[2]
    residual = source
    for k, dim in ((kx, 0), (ky, 1), (kz, 2)):
        for step in (1, -1):
            residual = residual - trans_of(k, shifted(k, dim, step)) * (
                pressure - shifted(pressure, dim, step)
            )
    own = scatter(basis, support, residual)

    def rows_of(edge, lo, acc_lo, m_lo):
        c = jnp.array([0, ny - 1])
        return [
            pressure[edge],
            kx[edge],
            saturation[edge],
            basis[edge],
            pressure[lo : lo + EDGE][:, c],
            ky[lo : lo + EDGE][:, c],
            basis[lo : lo + EDGE][:, c],
            support[lo : lo + EDGE],
            own[acc_lo : acc_lo + EDGE],
            matrix[:, m_lo : m_lo + REACH],
        ]

    first = rows_of(0, 0, 0, 0)
    last = rows_of(nx - 1, nx - EDGE, nx + 2 - EDGE, nx - REACH)
    before, after = exchange("narrow", pack(first), pack(last), True)
    before, after = unpack(before, last), unpack(after, first)

    tall = nx + 2 * REACH
    acc = jnp.pad(own, ((REACH - 1, REACH - 1), (0, 0)))
    acc = acc + jnp.pad(before[8], ((0, tall - EDGE), (0, 0)))
    acc = acc + jnp.pad(after[8], ((tall - EDGE, 0), (0, 0)))
    for edge, other, sup_row, other_row in ((0, before, EDGE - 1, -1), (nx - 1, after, 0, nx)):
        flux = trans_of(kx[edge], other[1]) * (pressure[edge] - other[0])
        for b, s, r, row in (
            (basis[edge], support[edge], -flux, edge),
            (other[3], other[7][sup_row], flux, other_row),
        ):
            put = scatter(b[None], s[None], r[None])
            top = REACH - 1 + row
            acc = acc + jnp.pad(put, ((top, tall - 3 - top), (0, 0)))
    mat = jnp.concatenate([before[9], matrix, after[9]], axis=1)
    sup = jnp.concatenate([before[7], support, after[7]], axis=0)

    def cols_of(c, at, acc_lo, m_lo):
        return [
            jnp.concatenate([before[4][:, at], pressure[:, c], after[4][:, at]]),
            jnp.concatenate([before[5][:, at], ky[:, c], after[5][:, at]]),
            jnp.concatenate([before[6][:, at], basis[:, c], after[6][:, at]]),
            sup[:, c],
            saturation[:, c],
            acc[:, acc_lo : acc_lo + EDGE],
            mat[:, :, m_lo : m_lo + REACH],
        ]

    leftmost = cols_of(0, 0, 0, 0)
    rightmost = cols_of(ny - 1, 1, ny + 2 - EDGE, ny - REACH)
    left, right = exchange("wide", pack(leftmost), pack(rightmost), False)
    left, right = unpack(left, rightmost), unpack(right, leftmost)

    wide = ny + 2 * REACH
    res = jnp.pad(acc, ((0, 0), (REACH - 1, REACH - 1)))
    res = res + jnp.pad(left[5], ((0, 0), (0, wide - EDGE)))
    res = res + jnp.pad(right[5], ((0, 0), (wide - EDGE, 0)))
    for mine, other, col, other_col in ((leftmost, left, 0, -1), (rightmost, right, ny - 1, ny)):
        flux = trans_of(mine[1], other[1]) * (mine[0] - other[0])
        for b, s, r, at in ((mine[2], mine[3], -flux, col), (other[2], other[3], flux, other_col)):
            put = scatter(b[:, None], s[:, None], r[:, None])[2:-2]
            start = REACH - 1 + at
            res = res + jnp.pad(put, ((0, 0), (start, wide - 3 - start)))
    mat = jnp.concatenate([left[6], mat, right[6]], axis=2)
    diag = mat[4]
    scale = jnp.where(diag > 0, OMEGA / jnp.where(diag > 0, diag, 1.0), 0.0)
    coarse = scale * res
    for _ in range(SWEEPS - 1):
        pad = jnp.pad(coarse, 1)
        total = res
        for o, (dx, dy) in enumerate(OFFSETS):
            total = total - mat[o] * pad[1 + dx : 1 + dx + tall, 1 + dy : 1 + dy + wide]
        coarse = coarse + scale * total

    new = corrected(pressure, basis, support, coarse, REACH, REACH)
    up = corrected(before[0][None], before[3][None], before[7][-1:], coarse, REACH - 1, REACH)
    down = corrected(after[0][None], after[3][None], after[7][:1], coarse, REACH + nx, REACH)
    mid = slice(EDGE, EDGE + nx)
    west = corrected(left[0][mid, None], left[2][mid, None], left[3][mid, None], coarse, REACH, REACH - 1)
    east = corrected(right[0][mid, None], right[2][mid, None], right[3][mid, None], coarse, REACH, REACH + ny)

    def padded(a, dim, lo, hi):
        return jnp.concatenate([lo, a, hi], axis=dim)

    none = jnp.zeros_like(pressure[:, :, :1])
    pads = (
        (0, (up, down), (before[1][None], after[1][None]), (before[2][None], after[2][None])),
        (1, (west, east), (left[1][mid, None], right[1][mid, None]), (left[4][:, None], right[4][:, None])),
        (2, (none, none), (none, none), (none, none)),
    )
    frac = fraction(saturation)
    total = jnp.zeros_like(pressure)
    for k, (dim, p_ends, k_ends, s_ends) in zip((kx, ky, kz), pads):
        n = pressure.shape[dim]
        p_pad = padded(new, dim, *p_ends)
        k_pad = padded(k, dim, *k_ends)
        f_pad = padded(frac, dim, fraction(s_ends[0]), fraction(s_ends[1]))
        for lo in (0, 2):
            take = lambda a: lax.slice_in_dim(a, lo, lo + n, axis=dim)
            flux = trans_of(k, take(k_pad)) * (new - take(p_pad))
            total = total + flux * jnp.where(flux > 0, frac, take(f_pad))
    return new, saturation - DT * total / pore_volume


def solution(mesh):
    return jax.shard_map(
        on_device,
        mesh=mesh,
        in_specs=(
            P("narrow", "wide", None),
            P("narrow", "wide", None),
            P("narrow", "wide", None),
            P(None, "narrow", "wide", None),
            P("narrow", "wide", None),
            P("narrow", "wide", None, None),
            P("narrow", "wide", None),
            P(None, "narrow", "wide"),
        ),
        out_specs=(P("narrow", "wide", None), P("narrow", "wide", None)),
        check_vma=False,
    )
```

```python
import jax
import jax.numpy as jnp
from jax import lax
from jax.experimental import pallas as pl
from jax.experimental.pallas import tpu as pltpu
from jax.sharding import PartitionSpec as P

SWEEPS = 3
OFFSETS = [(o // 3 - 1, o % 3 - 1) for o in range(9)]
OMEGA = 0.6667
DT = 0.01

NX, NY, L, K = 16, 32, 128, 4
TOP, WEST, TALL = 8, 4, 32
EDGE = 5
FIELDS = 2 + K
SUP, MAT, ACC = 0, K, K + 9
SMALL = K + 10
N_P, N_K, N_S, N_B, N_C = 0, 32, 64, 96, 224
N_SMALL = 288
N_ROWS = N_SMALL + 8 * 5
W_SAT = FIELDS * TALL
W_SMALL = W_SAT + NX
W_ROWS = W_SMALL + TALL


def roll(a, shift, axis):
    shift %= a.shape[axis]
    return pltpu.roll(a, shift, axis) if shift else a


def iota(shape, axis):
    return lax.broadcasted_iota(jnp.int32, shape, axis)


def trans_of(here, there):
    return 2.0 * here * there / (here + there)


def fraction(sat):
    rest = 1.0 - sat
    square = sat * sat
    return square / (square + 0.5 * (rest * rest))


def lane_sum(a):
    return jnp.sum(a, axis=-1, keepdims=True)


def bin_pieces(sup, pieces):
    total = None
    for dy in (-1, 0, 1):
        column = None
        for dx in (-1, 0, 1):
            code = float((dx + 1) * 3 + dy + 1)
            part = None
            for k in range(K):
                term = jnp.where(sup[k] == code, pieces[k], 0.0)
                part = term if part is None else part + term
            part = roll(part, dx, 0)
            column = part if column is None else column + part
        column = roll(column, dy, 1)
        total = column if total is None else total + column
    return total


def turned(scratch, value):
    scratch[...] = jnp.zeros((L, L), jnp.float32)
    scratch[WEST : WEST + NY, :] = value
    return scratch[...].T


def residual_kernel(
    p, sat, src, perm, basis, support, matrix, out_even, out_odd, small, bs, place, square
):
    even = lax.axis_index("narrow") % 2 == 0
    lanes = iota((NY, L), 1)
    rows = iota((NY, L), 0)
    cells = NX * NY
    div = [None] * NX
    last_x = None
    for x in range(NX):
        at = slice(x * NY, (x + 1) * NY)
        here = p[at, :]
        kx, ky, kz = (perm[c * cells + x * NY : c * cells + (x + 1) * NY, :] for c in range(3))
        fy = trans_of(ky, roll(ky, -1, 0)) * (here - roll(here, -1, 0))
        fy = jnp.where(rows < NY - 1, fy, 0.0)
        fz = trans_of(kz, roll(kz, -1, 1)) * (here - roll(here, -1, 1))
        fz = jnp.where(lanes < L - 1, fz, 0.0)
        total = (fy - roll(fy, 1, 0)) + (fz - roll(fz, 1, 1))
        if x < NX - 1:
            fx = trans_of(kx, perm[(x + 1) * NY : (x + 2) * NY, :]) * (here - p[(x + 1) * NY : (x + 2) * NY, :])
            total = total + fx
        if last_x is not None:
            total = total - last_x
        last_x = fx
        div[x] = total
    pieces = jnp.zeros((NY, L), jnp.float32)
    for x in range(NX):
        at = slice(x * NY * K, (x + 1) * NY * K)
        bs[at, :] = basis[at, :].astype(jnp.float32)
        res = src[x * NY : (x + 1) * NY, :] - div[x]
        for k in range(K):
            b = bs[pl.ds(x * NY * K + k, NY, stride=K), :]
            pieces = jnp.where(lanes == k * TALL + TOP + x, lane_sum(b * res), pieces)
    flipped = turned(square, pieces)
    place[...] = jnp.zeros((TALL, L), jnp.float32)
    stack = []
    for i in range(K + 9):
        if i < MAT:
            value = support[pl.ds(i, NX, stride=K), :].astype(jnp.float32)
        else:
            value = matrix[(i - MAT) * NX : (i - MAT + 1) * NX, :]
        place[TOP : TOP + NX, 0:NY] = value
        stack.append(roll(place[...], WEST, 1))
    acc = bin_pieces(stack[:K], [flipped[k * TALL : (k + 1) * TALL, :] for k in range(K)])
    stack.append(acc)
    for i in range(SMALL):
        small[i * TALL : (i + 1) * TALL, :] = stack[i]
    for out, takes_last in ((out_even, even), (out_odd, jnp.logical_not(even))):
        edge = jnp.where(takes_last, NX - 1, 0)
        row = pl.multiple_of(edge * NY, NY)
        out[N_P : N_P + NY, :] = p[pl.ds(row, NY), :]
        out[N_K : N_K + NY, :] = perm[pl.ds(row, NY), :]
        out[N_S : N_S + NY, :] = sat[pl.ds(row, NY), :]
        for k in range(K):
            out[N_B + k * NY : N_B + (k + 1) * NY, :] = bs[pl.ds(row * K + k, NY, stride=K), :]
        start = jnp.where(takes_last, NX - EDGE, 0) * NY
        for c, col in enumerate((0, NY - 1)):
            fields = [
                p[pl.ds(start + col, EDGE, stride=NY), :],
                perm[pl.ds(start + (cells + col), EDGE, stride=NY), :],
            ] + [bs[pl.ds((start + col) * K + k, EDGE, stride=NY * K), :] for k in range(K)]
            for f, value in enumerate(fields):
                to = N_C + (f * 2 + c) * EDGE
                out[to : to + EDGE, :] = value
        window = [jnp.where(takes_last, s[16:24, :], s[8:16, :]) for s in stack]
        window.append(jnp.where(takes_last, acc[24:32, :], acc[0:8, :]))
        for i in range(5):
            a, b, c = window[3 * i : 3 * i + 3]
            out[N_SMALL + 8 * i : N_SMALL + 8 * i + 8, :] = a + roll(b, 40, 1) + roll(c, 80, 1)


def narrow_kernel(
    gathered, odd, p, sat, perm, bs, small, out_even, out_odd, small_out, square
):
    even = lax.axis_index("narrow") % 2 == 0
    wide_even = lax.axis_index("wide") % 2 == 0
    mate = jnp.where(even, 1, 0)
    cells = NX * NY
    lanes = iota((NY, L), 1)

    def before(lo, n):
        return jnp.where(even, odd[lo : lo + n, :], gathered[mate, lo : lo + n, :])

    def after(lo, n):
        return jnp.where(even, gathered[mate, lo : lo + n, :], odd[lo : lo + n, :])

    in_slot = iota((8, L), 1) < 40

    def windows(get):
        out = []
        for i in range(5):
            block = get(N_SMALL + 8 * i, 8)
            out += [jnp.where(in_slot, roll(block, -40 * j, 1), 0.0) for j in range(3)]
        return out

    top, bottom = windows(before), windows(after)
    none = jnp.zeros((8, L), jnp.float32)
    stack = []
    for i in range(SMALL):
        own = small[i * TALL : (i + 1) * TALL, :]
        if i < ACC:
            own = own[8:24, :]
            stack.append(jnp.concatenate([top[i], own, bottom[i]], axis=0))
        else:
            stack.append(own + jnp.concatenate([top[i], top[i + 1], bottom[i + 1], bottom[i]], axis=0))
    pieces = jnp.zeros((NY, L), jnp.float32)
    for x, other_x, get in ((0, -1, before), (NX - 1, NX, after)):
        at = x * NY
        flux = trans_of(perm[at : at + NY, :], get(N_K, NY)) * (p[at : at + NY, :] - get(N_P, NY))
        for k in range(K):
            mine = lane_sum(bs[pl.ds(at * K + k, NY, stride=K), :] * -flux)
            pieces = jnp.where(lanes == k * TALL + TOP + x, mine, pieces)
            other = lane_sum(get(N_B + k * NY, NY) * flux)
            pieces = jnp.where(lanes == k * TALL + TOP + other_x, other, pieces)
    flipped = turned(square, pieces)
    stack[ACC] = stack[ACC] + bin_pieces(
        stack[:K], [flipped[k * TALL : (k + 1) * TALL, :] for k in range(K)]
    )
    for i in range(SMALL):
        small_out[i * TALL : (i + 1) * TALL, :] = stack[i]
    slot = iota((TALL, L), 1) // 8
    first = jnp.zeros((TALL, L), jnp.float32)
    last = jnp.zeros((TALL, L), jnp.float32)
    for i in range(SMALL):
        first = jnp.where(slot == i, roll(stack[i], 8 * i, 1), first)
        last = jnp.where(slot == i, roll(stack[i], 8 * i - 32, 1), last)
    blank = jnp.zeros((8, L), jnp.float32)
    for out, takes_last in ((out_even, wide_even), (out_odd, jnp.logical_not(wide_even))):
        col = jnp.where(takes_last, NY - 1, 0)
        fields = [
            p[pl.ds(col, NX, stride=NY), :],
            perm[pl.ds(cells + col, NX, stride=NY), :],
        ] + [bs[pl.ds(col * K + k, NX, stride=NY * K), :] for k in range(K)]
        for f, value in enumerate(fields):
            base = f * TALL
            lo = N_C + f * 2 * EDGE
            out[base : base + 8, :] = blank
            out[base + 24 : base + 32, :] = blank
            out[base + 3 : base + 8, :] = jnp.where(takes_last, before(lo + EDGE, EDGE), before(lo, EDGE))
            out[base + 8 : base + 24, :] = value
            out[base + 24 : base + 29, :] = jnp.where(takes_last, after(lo + EDGE, EDGE), after(lo, EDGE))
        out[W_SAT : W_SAT + NX, :] = sat[pl.ds(col, NX, stride=NY), :]
        out[W_SMALL : W_SMALL + TALL, :] = jnp.where(takes_last, last, first)


def final_kernel(
    in_even, in_odd, sent_even, sent_odd, gathered, odd, small, p, sat, perm, pore, bs, new, new_sat, square
):
    even = lax.axis_index("narrow") % 2 == 0
    wide_even = lax.axis_index("wide") % 2 == 0
    mate = jnp.where(even, 1, 0)
    cells = NX * NY

    def before(lo, n):
        return jnp.where(even, odd[lo : lo + n, :], gathered[mate, lo : lo + n, :])

    def after(lo, n):
        return jnp.where(even, gathered[mate, lo : lo + n, :], odd[lo : lo + n, :])

    def left(lo, n):
        return jnp.where(wide_even, in_odd[lo : lo + n, :], in_even[lo : lo + n, :])

    def right(lo, n):
        return jnp.where(wide_even, in_even[lo : lo + n, :], in_odd[lo : lo + n, :])

    def first(lo, n):
        return jnp.where(wide_even, sent_odd[lo : lo + n, :], sent_even[lo : lo + n, :])

    def last(lo, n):
        return jnp.where(wide_even, sent_even[lo : lo + n, :], sent_odd[lo : lo + n, :])

    lane = iota((TALL, L), 1)
    from_left, from_right = left(W_SMALL, TALL), right(W_SMALL, TALL)
    stack = []
    for i in range(SMALL):
        own = small[i * TALL : (i + 1) * TALL, :]
        own = own + jnp.where(lane < 8, roll(from_left, -8 * i, 1), 0.0)
        own = own + jnp.where(lane // 8 == 4, roll(from_right, 32 - 8 * i, 1), 0.0)
        stack.append(own)
    sup, mat = stack[:K], stack[MAT : MAT + 9]
    pieces = [jnp.zeros((TALL, L), jnp.float32)] * K
    for mine, other, y, other_y in ((first, left, 0, -1), (last, right, NY - 1, NY)):
        k_here, k_there = mine(TALL, TALL), other(TALL, TALL)
        total = k_here + k_there
        flux = (2.0 * k_here * k_there / jnp.where(total > 0, total, 1.0)) * (mine(0, TALL) - other(0, TALL))
        for k in range(K):
            lo = (2 + k) * TALL
            here = lane_sum(mine(lo, TALL) * -flux)
            there = lane_sum(other(lo, TALL) * flux)
            pieces[k] = jnp.where(lane == WEST + y, here, pieces[k])
            pieces[k] = jnp.where(lane == WEST + other_y, there, pieces[k])
    res = stack[ACC] + bin_pieces(sup, pieces)
    diag = mat[4]
    scale = jnp.where(diag > 0, OMEGA / jnp.where(diag > 0, diag, 1.0), 0.0)

    def moved(coarse):
        sides = {dy: roll(coarse, -dy, 1) for dy in (-1, 0, 1)}
        return [roll(sides[dy], -dx, 0) for dx, dy in OFFSETS]

    coarse = scale * res
    for _ in range(SWEEPS - 1):
        rest = res
        for o, value in enumerate(moved(coarse)):
            rest = rest - mat[o] * value
        coarse = coarse + scale * rest
    shifts = moved(coarse)
    picked = []
    for k in range(K):
        total = jnp.zeros((TALL, L), jnp.float32)
        for o in range(9):
            total = jnp.where(sup[k] == float(o), shifts[o], total)
        picked.append(total)
    for k in range(K):
        square[k * TALL : (k + 1) * TALL, :] = roll(picked[k], -WEST, 1)
    weights = square[...].T[0:NY, :]

    def weight(k, x):
        at = k * TALL + TOP + x
        return weights[:, at : at + 1]

    for x in range(NX):
        at = slice(x * NY, (x + 1) * NY)
        total = p[at, :]
        for k in range(K):
            total = total + bs[pl.ds(x * NY * K + k, NY, stride=K), :] * weight(k, x)
        new[at, :] = total
    ends = []
    for get, x in ((before, -1), (after, NX)):
        total = get(N_P, NY)
        for k in range(K):
            total = total + get(N_B + k * NY, NY) * weight(k, x)
        ends.append(total)
    sides = []
    for get, y in ((left, -1), (right, NY)):
        total = get(TOP, NX)
        for k in range(K):
            column = picked[k][TOP : TOP + NX, WEST + y : WEST + y + 1]
            total = total + get((2 + k) * TALL + TOP, NX) * column
        sides.append(total)

    def carried(trans, here, there, f_here, f_there):
        flux = trans * (here - there)
        return flux * jnp.where(flux > 0, f_here, f_there)

    west_k, east_k = left(TALL + TOP, NX), right(TALL + TOP, NX)
    west_f, east_f = fraction(left(W_SAT, NX)), fraction(right(W_SAT, NX))
    first_k = perm[pl.ds(cells, NX, stride=NY), :]
    west_flow = carried(
        trans_of(west_k, first_k),
        sides[0],
        new[pl.ds(0, NX, stride=NY), :],
        west_f,
        fraction(sat[pl.ds(0, NX, stride=NY), :]),
    )
    rows = iota((NY, L), 0)
    lanes = iota((NY, L), 1)
    kx_prev = before(N_K, NY)
    p_here, f_here, kx = new[0:NY, :], fraction(sat[0:NY, :]), perm[0:NY, :]
    flow_in = carried(trans_of(kx_prev, kx), ends[0], p_here, fraction(before(N_S, NY)), f_here)
    for x in range(NX):
        at = slice(x * NY, (x + 1) * NY)
        if x < NX - 1:
            nxt = slice((x + 1) * NY, (x + 2) * NY)
            p_next, f_next, kx_next = new[nxt, :], fraction(sat[nxt, :]), perm[nxt, :]
        else:
            p_next, f_next, kx_next = ends[1], fraction(after(N_S, NY)), after(N_K, NY)
        flow_out = carried(trans_of(kx, kx_next), p_here, p_next, f_here, f_next)
        total = flow_out - flow_in
        flow_in = flow_out
        ky = perm[cells + x * NY : cells + (x + 1) * NY, :]
        end = rows == NY - 1
        beside = lambda a, e: jnp.where(end, e[x : x + 1, :], roll(a, -1, 0))
        fy = carried(
            trans_of(ky, beside(ky, east_k)), p_here, beside(p_here, sides[1]), f_here, beside(f_here, east_f)
        )
        total = total + (fy - jnp.where(rows == 0, west_flow[x : x + 1, :], roll(fy, 1, 0)))
        kz = perm[2 * cells + x * NY : 2 * cells + (x + 1) * NY, :]
        fz = carried(
            trans_of(kz, roll(kz, -1, 1)), p_here, roll(p_here, -1, 1), f_here, roll(f_here, -1, 1)
        )
        fz = jnp.where(lanes < L - 1, fz, 0.0)
        total = total + (fz - roll(fz, 1, 1))
        new_sat[at, :] = sat[at, :] - DT * total / pore[at, :]
        p_here, f_here, kx = p_next, f_next, kx_next


def call(kernel, out_rows, scratch, flops, *args):
    shapes = [jax.ShapeDtypeStruct((r, L), jnp.float32) for r in out_rows]
    size = sum(a.size * a.dtype.itemsize for a in args) + sum(4 * L * r for r in out_rows)
    return pl.pallas_call(
        kernel,
        out_shape=shapes,
        in_specs=[pl.BlockSpec(memory_space=pltpu.VMEM)] * len(args),
        out_specs=[pl.BlockSpec(memory_space=pltpu.VMEM)] * len(shapes),
        scratch_shapes=[pltpu.VMEM((r, L), jnp.float32) for r in scratch],
        compiler_params=pltpu.CompilerParams(vmem_limit_bytes=32 * 1024 * 1024),
        cost_estimate=pl.CostEstimate(flops=flops, bytes_accessed=size, transcendentals=0),
    )(*args)


def swaps(n, start):
    pairs = [(i, i + 1) for i in range(start, n - 1, 2)]
    return pairs + [(j, i) for i, j in pairs]


def on_device(pressure, saturation, source, perm, pore_volume, basis, support, matrix):
    p, sat, src, k, pore = (
        a.reshape(-1, L) for a in (pressure, saturation, source, perm, pore_volume)
    )
    basis = basis.reshape(-1, L)
    support = support.transpose(0, 2, 1).reshape(NX * K, NY)
    matrix = matrix.reshape(9 * NX, NY)
    n_narrow, n_wide = lax.axis_size("narrow"), lax.axis_size("wide")
    out_even, out_odd, small, bs = call(
        residual_kernel, [N_ROWS, N_ROWS, SMALL * TALL, NX * NY * K], [TALL, L], 10**7,
        p, sat, src, k, basis, support, matrix,
    )
    odd = lax.ppermute(out_odd, "narrow", swaps(n_narrow, 1))
    gathered = lax.all_gather(
        out_even, "narrow", axis_index_groups=[[i, i + 1] for i in range(0, n_narrow, 2)]
    )
    sent_even, sent_odd, small = call(
        narrow_kernel, [W_ROWS, W_ROWS, SMALL * TALL], [L], 10**6,
        gathered, odd, p, sat, k, bs, small,
    )
    in_odd = lax.ppermute(sent_odd, "wide", swaps(n_wide, 1))
    in_even = lax.ppermute(sent_even, "wide", swaps(n_wide, 0))
    new, new_sat = call(
        final_kernel, [NX * NY, NX * NY], [L], 10**7,
        in_even, in_odd, sent_even, sent_odd, gathered, odd, small, p, sat, k, pore, bs,
    )
    return new.reshape(pressure.shape), new_sat.reshape(pressure.shape)


def solution(mesh):
    return jax.shard_map(
        on_device,
        mesh=mesh,
        in_specs=(
            P("narrow", "wide", None),
            P("narrow", "wide", None),
            P("narrow", "wide", None),
            P(None, "narrow", "wide", None),
            P("narrow", "wide", None),
            P("narrow", "wide", None, None),
            P("narrow", "wide", None),
            P(None, "narrow", "wide"),
        ),
        out_specs=(P("narrow", "wide", None), P("narrow", "wide", None)),
        check_vma=False,
    )
```

```python
import jax
import jax.numpy as jnp
from jax import lax
from jax.experimental import pallas as pl
from jax.experimental.pallas import tpu as pltpu
from jax.sharding import PartitionSpec as P

SWEEPS = 3
OFFSETS = [(o // 3 - 1, o % 3 - 1) for o in range(9)]
OMEGA = 0.6667
DT = 0.01

NX, NY, L, K = 16, 32, 128, 4
TOP, WEST, TALL = 8, 4, 32
EDGE = 5
FIELDS = 2 + K
SUP, MAT, ACC = 0, K, K + 9
SMALL = K + 10
N_P, N_K, N_S, N_B, N_C = 0, 32, 64, 96, 224
N_SMALL = 288
N_ROWS = N_SMALL + 8 * 5
W_SAT = FIELDS * TALL
W_SMALL = W_SAT + NX
W_ROWS = W_SMALL + TALL


def roll(a, shift, axis):
    shift %= a.shape[axis]
    return pltpu.roll(a, shift, axis) if shift else a


def iota(shape, axis):
    return lax.broadcasted_iota(jnp.int32, shape, axis)


def trans_of(here, there):
    return 2.0 * here * there / (here + there)


def fraction(sat):
    rest = 1.0 - sat
    square = sat * sat
    return square / (square + 0.5 * (rest * rest))


def lane_sum(a):
    return jnp.sum(a, axis=-1, keepdims=True)


def bin_pieces(sup, pieces):
    total = None
    for dy in (-1, 0, 1):
        column = None
        for dx in (-1, 0, 1):
            code = float((dx + 1) * 3 + dy + 1)
            part = None
            for k in range(K):
                term = jnp.where(sup[k] == code, pieces[k], 0.0)
                part = term if part is None else part + term
            part = roll(part, dx, 0)
            column = part if column is None else column + part
        column = roll(column, dy, 1)
        total = column if total is None else total + column
    return total


def turned(scratch, value):
    scratch[...] = jnp.zeros((L, L), jnp.float32)
    scratch[WEST : WEST + NY, :] = value
    return scratch[...].T


def rows_residual(p, perm, src, trans, lo, hi, base):
    rows, lanes = iota((NY, L), 0), iota((NY, L), 1)

    def face(x):
        a, b = slice(x * NY, (x + 1) * NY), slice((x + 1) * NY, (x + 2) * NY)
        value = trans_of(perm[0, a, :], perm[0, b, :])
        if x >= lo:
            trans[0, (x - base) * NY : (x - base + 1) * NY, :] = value
        return value * (p[a, :] - p[b, :])

    result = []
    last = face(lo - 1) if lo > 0 else None
    for x in range(lo, hi):
        at = slice(x * NY, (x + 1) * NY)
        here, ky, kz = p[at, :], perm[1, at, :], perm[2, at, :]
        ty = jnp.where(rows < NY - 1, trans_of(ky, roll(ky, -1, 0)), 0.0)
        tz = jnp.where(lanes < L - 1, trans_of(kz, roll(kz, -1, 1)), 0.0)
        to = slice((x - base) * NY, (x - base + 1) * NY)
        trans[1, to, :] = ty
        trans[2, to, :] = tz
        fy = ty * (here - roll(here, -1, 0))
        fz = tz * (here - roll(here, -1, 1))
        total = (fy - roll(fy, 1, 0)) + (fz - roll(fz, 1, 1))
        if last is not None:
            total = total - last
        last = None
        if x < NX - 1:
            last = face(x)
            total = total + last
        result.append(src[to, :] - total)
    return result


def add_pieces(pieces, residuals, lo, bs, base):
    lanes = iota((NY, L), 1)
    for i, res in enumerate(residuals):
        x = lo + i
        for k in range(K):
            b = bs[pl.ds((x - base) * NY * K + k, NY, stride=K), :]
            pieces = jnp.where(lanes == k * TALL + TOP + x, lane_sum(b * res), pieces)
    return pieces


def split_pieces(square, pieces):
    flipped = turned(square, pieces)
    return [flipped[k * TALL : (k + 1) * TALL, :] for k in range(K)]


LIMIT1 = 24
LOW, HIGH = EDGE, NX - EDGE


def copies_of(sems, pairs):
    out = [pltpu.make_async_copy(src, dst, sems.at[i]) for i, (src, dst) in enumerate(pairs)]
    for copy in out:
        copy.start()
    return out


def edge_kernel(
    p_in, perm_in, src_in, basis_in, support_in, matrix_in, sat_in,
    out_even, out_odd, small, p, perm, sat, bs, trans,
    src, basis, support, matrix, place, square, sems,
):
    even = lax.axis_index("narrow") % 2 == 0
    top, bottom, middle = (
        pl.ds(0, (LOW + 1) * NY),
        pl.ds((HIGH - 1) * NY, (LOW + 1) * NY),
        pl.ds((LOW + 1) * NY, (HIGH - LOW - 2) * NY),
    )
    pairs = []
    for part, first in ((top, 0), (bottom, HIGH)):
        own, fine = pl.ds(first * NY, EDGE * NY), pl.ds(first * NY * K, EDGE * NY * K)
        pairs += [(p_in.at[part], p.at[part]), (perm_in.at[:, part], perm.at[:, part])]
        pairs += [(src_in.at[own], src.at[own]), (basis_in.at[fine], basis.at[fine])]
    pairs += [(support_in, support), (matrix_in, matrix), (sat_in, sat)]
    pairs += [(p_in.at[middle], p.at[middle]), (perm_in.at[:, middle], perm.at[:, middle])]
    copies = copies_of(sems, pairs)
    pieces = jnp.zeros((NY, L), jnp.float32)
    for i, first in enumerate((0, HIGH)):
        for copy in copies[4 * i : 4 * i + 3]:
            copy.wait()
        residuals = rows_residual(p, perm, src, trans, first, first + EDGE, 0)
        copies[4 * i + 3].wait()
        fine = slice(first * NY * K, (first + EDGE) * NY * K)
        bs[fine, :] = basis[fine, :].astype(jnp.float32)
        pieces = add_pieces(pieces, residuals, first, bs, 0)
    pieces = split_pieces(square, pieces)
    copies[8].wait()
    copies[9].wait()
    place[...] = jnp.zeros((TALL, L), jnp.float32)
    stack = []
    for i in range(K + 9):
        if i < MAT:
            value = support[pl.ds(i, NX, stride=K), :].astype(jnp.float32)
        else:
            value = matrix[(i - MAT) * NX : (i - MAT + 1) * NX, :]
        place[TOP : TOP + NX, 0:NY] = value
        stack.append(roll(place[...], WEST, 1))
    acc = bin_pieces(stack[:K], pieces)
    stack.append(acc)
    for i in range(SMALL):
        small[i * TALL : (i + 1) * TALL, :] = stack[i]
    copies[10].wait()
    for out, takes_last in ((out_even, even), (out_odd, jnp.logical_not(even))):
        edge = jnp.where(takes_last, NX - 1, 0)
        row = pl.multiple_of(edge * NY, NY)
        out[N_P : N_P + NY, :] = p[pl.ds(row, NY), :]
        out[N_K : N_K + NY, :] = perm[0, pl.ds(row, NY), :]
        out[N_S : N_S + NY, :] = sat[pl.ds(row, NY), :]
        for k in range(K):
            out[N_B + k * NY : N_B + (k + 1) * NY, :] = bs[pl.ds(row * K + k, NY, stride=K), :]
        start = jnp.where(takes_last, NX - EDGE, 0) * NY
        for c, col in enumerate((0, NY - 1)):
            fields = [
                p[pl.ds(start + col, EDGE, stride=NY), :],
                perm[1, pl.ds(start + col, EDGE, stride=NY), :],
            ] + [bs[pl.ds((start + col) * K + k, EDGE, stride=NY * K), :] for k in range(K)]
            for f, value in enumerate(fields):
                to = N_C + (f * 2 + c) * EDGE
                out[to : to + EDGE, :] = value
        window = [jnp.where(takes_last, s[16:24, :], s[8:16, :]) for s in stack]
        window.append(jnp.where(takes_last, acc[24:32, :], acc[0:8, :]))
        for i in range(5):
            a, b, c = window[3 * i : 3 * i + 3]
            out[N_SMALL + 8 * i : N_SMALL + 8 * i + 8, :] = a + roll(b, 40, 1) + roll(c, 80, 1)
    copies[11].wait()
    copies[12].wait()


def middle_kernel(
    src_in, basis_in, pore_in, p, perm, sat, small,
    bs, trans, acc, frac, rate,
    src, basis, pore, square, sems,
):
    own, fine = pl.ds(LOW * NY, (HIGH - LOW) * NY), pl.ds(LOW * NY * K, (HIGH - LOW) * NY * K)
    copies = copies_of(sems, [(src_in.at[own], src), (basis_in.at[fine], basis), (pore_in, pore)])
    frac[...] = fraction(sat[...])
    copies[0].wait()
    residuals = rows_residual(p, perm, src, trans, LOW, HIGH, LOW)
    copies[1].wait()
    bs[...] = basis[...].astype(jnp.float32)
    pieces = add_pieces(jnp.zeros((NY, L), jnp.float32), residuals, LOW, bs, LOW)
    sup = [small[k * TALL : (k + 1) * TALL, :] for k in range(K)]
    acc[...] = bin_pieces(sup, split_pieces(square, pieces))
    copies[2].wait()
    rate[...] = DT / pore[...]


def narrow_kernel(
    gathered, odd, p, sat, perm, bs, bs_middle, small, acc_middle, out_odd, out_even, small_out, square
):
    even = lax.axis_index("narrow") % 2 == 0
    wide_even = lax.axis_index("wide") % 2 == 0
    mate = jnp.where(even, 1, 0)
    lanes = iota((NY, L), 1)

    def before(lo, n):
        return jnp.where(even, odd[lo : lo + n, :], gathered[mate, lo : lo + n, :])

    def after(lo, n):
        return jnp.where(even, gathered[mate, lo : lo + n, :], odd[lo : lo + n, :])

    in_slot = iota((8, L), 1) < 40

    def windows(get):
        out = []
        for i in range(5):
            block = get(N_SMALL + 8 * i, 8)
            out += [jnp.where(in_slot, roll(block, -40 * j, 1), 0.0) for j in range(3)]
        return out

    top, bottom = windows(before), windows(after)
    none = jnp.zeros((8, L), jnp.float32)
    stack = []
    for i in range(SMALL):
        own = small[i * TALL : (i + 1) * TALL, :]
        if i < ACC:
            own = own[8:24, :]
            stack.append(jnp.concatenate([top[i], own, bottom[i]], axis=0))
        else:
            stack.append(own + jnp.concatenate([top[i], top[i + 1], bottom[i + 1], bottom[i]], axis=0))
    pieces = jnp.zeros((NY, L), jnp.float32)
    for x, other_x, get in ((0, -1, before), (NX - 1, NX, after)):
        at = x * NY
        flux = trans_of(perm[0, at : at + NY, :], get(N_K, NY)) * (p[at : at + NY, :] - get(N_P, NY))
        for k in range(K):
            mine = lane_sum(bs[pl.ds(at * K + k, NY, stride=K), :] * -flux)
            pieces = jnp.where(lanes == k * TALL + TOP + x, mine, pieces)
            other = lane_sum(get(N_B + k * NY, NY) * flux)
            pieces = jnp.where(lanes == k * TALL + TOP + other_x, other, pieces)
    stack[ACC] = stack[ACC] + acc_middle[...] + bin_pieces(stack[:K], split_pieces(square, pieces))
    for i in range(SMALL):
        small_out[i * TALL : (i + 1) * TALL, :] = stack[i]
    slot = iota((TALL, L), 1) // 8
    first = jnp.zeros((TALL, L), jnp.float32)
    last = jnp.zeros((TALL, L), jnp.float32)
    for i in range(SMALL):
        first = jnp.where(slot == i, roll(stack[i], 8 * i, 1), first)
        last = jnp.where(slot == i, roll(stack[i], 8 * i - 32, 1), last)
    blank = jnp.zeros((8, L), jnp.float32)
    for out, takes_last in ((out_even, wide_even), (out_odd, jnp.logical_not(wide_even))):
        col = jnp.where(takes_last, NY - 1, 0)
        for f in range(FIELDS):
            base = f * TALL
            lo = N_C + f * 2 * EDGE
            out[base : base + 8, :] = blank
            out[base + 24 : base + 32, :] = blank
            out[base + 3 : base + 8, :] = jnp.where(takes_last, before(lo + EDGE, EDGE), before(lo, EDGE))
            if f < 2:
                field = p[pl.ds(col, NX, stride=NY), :] if f == 0 else perm[1, pl.ds(col, NX, stride=NY), :]
                out[base + TOP : base + TOP + NX, :] = field
            else:
                at = col * K + f - 2
                for ref, x, start, n in (
                    (bs, 0, 0, LOW), (bs_middle, LOW, 0, HIGH - LOW), (bs, HIGH, HIGH, NX - HIGH)
                ):
                    column = ref[pl.ds(start * NY * K + at, n, stride=NY * K), :]
                    out[base + TOP + x : base + TOP + x + n, :] = column
            out[base + 24 : base + 29, :] = jnp.where(takes_last, after(lo + EDGE, EDGE), after(lo, EDGE))
        out[W_SAT : W_SAT + NX, :] = sat[pl.ds(col, NX, stride=NY), :]
        out[W_SMALL : W_SMALL + TALL, :] = jnp.where(takes_last, last, first)


def final_kernel(
    in_odd, in_even, sent_odd, sent_even, gathered, odd, small, p, sat, perm, bs, trans, bs_middle, trans_middle, frac, rate,
    new_out, new_sat_out,
    new, new_sat, square, sems,
):
    even = lax.axis_index("narrow") % 2 == 0
    wide_even = lax.axis_index("wide") % 2 == 0
    mate = jnp.where(even, 1, 0)

    def before(lo, n):
        return jnp.where(even, odd[lo : lo + n, :], gathered[mate, lo : lo + n, :])

    def after(lo, n):
        return jnp.where(even, gathered[mate, lo : lo + n, :], odd[lo : lo + n, :])

    def left(lo, n):
        return jnp.where(wide_even, in_odd[lo : lo + n, :], in_even[lo : lo + n, :])

    def right(lo, n):
        return jnp.where(wide_even, in_even[lo : lo + n, :], in_odd[lo : lo + n, :])

    def first(lo, n):
        return jnp.where(wide_even, sent_odd[lo : lo + n, :], sent_even[lo : lo + n, :])

    def last(lo, n):
        return jnp.where(wide_even, sent_even[lo : lo + n, :], sent_odd[lo : lo + n, :])

    lane = iota((TALL, L), 1)
    from_left, from_right = left(W_SMALL, TALL), right(W_SMALL, TALL)
    stack = []
    for i in range(SMALL):
        own = small[i * TALL : (i + 1) * TALL, :]
        own = own + jnp.where(lane < 8, roll(from_left, -8 * i, 1), 0.0)
        own = own + jnp.where(lane // 8 == 4, roll(from_right, 32 - 8 * i, 1), 0.0)
        stack.append(own)
    sup, mat = stack[:K], stack[MAT : MAT + 9]
    pieces = [jnp.zeros((TALL, L), jnp.float32)] * K
    for mine, other, y, other_y in ((first, left, 0, -1), (last, right, NY - 1, NY)):
        k_here, k_there = mine(TALL, TALL), other(TALL, TALL)
        total = k_here + k_there
        flux = (2.0 * k_here * k_there / jnp.where(total > 0, total, 1.0)) * (mine(0, TALL) - other(0, TALL))
        for k in range(K):
            lo = (2 + k) * TALL
            here = lane_sum(mine(lo, TALL) * -flux)
            there = lane_sum(other(lo, TALL) * flux)
            pieces[k] = jnp.where(lane == WEST + y, here, pieces[k])
            pieces[k] = jnp.where(lane == WEST + other_y, there, pieces[k])
    res = stack[ACC] + bin_pieces(sup, pieces)
    diag = mat[4]
    scale = jnp.where(diag > 0, OMEGA / jnp.where(diag > 0, diag, 1.0), 0.0)

    def moved(coarse):
        sides = {dy: roll(coarse, -dy, 1) for dy in (-1, 0, 1)}
        return [roll(sides[dy], -dx, 0) for dx, dy in OFFSETS]

    coarse = scale * res
    for _ in range(SWEEPS - 1):
        rest = res
        for o, value in enumerate(moved(coarse)):
            rest = rest - mat[o] * value
        coarse = coarse + scale * rest
    shifts = moved(coarse)
    picked = []
    for k in range(K):
        total = jnp.zeros((TALL, L), jnp.float32)
        for o in range(9):
            total = jnp.where(sup[k] == float(o), shifts[o], total)
        picked.append(total)
    for k in range(K):
        square[k * TALL : (k + 1) * TALL, :] = roll(picked[k], -WEST, 1)
    weights = square[...].T[0:NY, :]

    def weight(k, x):
        at = k * TALL + TOP + x
        return weights[:, at : at + 1]

    for x in range(NX):
        at = slice(x * NY, (x + 1) * NY)
        total = p[at, :]
        ref, base = (bs_middle, LOW) if LOW <= x < HIGH else (bs, 0)
        for k in range(K):
            total = total + ref[pl.ds((x - base) * NY * K + k, NY, stride=K), :] * weight(k, x)
        new[at, :] = total
    copies = copies_of(sems, [(new, new_out)])
    ends = []
    for get, x in ((before, -1), (after, NX)):
        total = get(N_P, NY)
        for k in range(K):
            total = total + get(N_B + k * NY, NY) * weight(k, x)
        ends.append(total)
    sides = []
    for get, y in ((left, -1), (right, NY)):
        total = get(TOP, NX)
        for k in range(K):
            column = picked[k][TOP : TOP + NX, WEST + y : WEST + y + 1]
            total = total + get((2 + k) * TALL + TOP, NX) * column
        sides.append(total)

    def carried(value, here, there, f_here, f_there):
        flux = value * (here - there)
        return flux * jnp.where(flux > 0, f_here, f_there)

    west_f, east_f = fraction(left(W_SAT, NX)), fraction(right(W_SAT, NX))
    east_t = trans_of(perm[1, pl.ds(NY - 1, NX, stride=NY), :], right(TALL + TOP, NX))
    west_flow = carried(
        trans_of(perm[1, pl.ds(0, NX, stride=NY), :], left(TALL + TOP, NX)),
        sides[0],
        new[pl.ds(0, NX, stride=NY), :],
        west_f,
        frac[pl.ds(0, NX, stride=NY), :],
    )
    rows = iota((NY, L), 0)
    end = rows == NY - 1
    p_here, f_here = new[0:NY, :], frac[0:NY, :]
    flow_in = carried(
        trans_of(before(N_K, NY), perm[0, 0:NY, :]), ends[0], p_here, fraction(before(N_S, NY)), f_here
    )
    for x in range(NX):
        at = slice(x * NY, (x + 1) * NY)
        ref, base = (trans_middle, LOW) if LOW <= x < HIGH else (trans, 0)
        tx, ty, tz = (ref[c, (x - base) * NY : (x - base + 1) * NY, :] for c in range(3))
        if x < NX - 1:
            nxt = slice((x + 1) * NY, (x + 2) * NY)
            p_next, f_next = new[nxt, :], frac[nxt, :]
        else:
            p_next, f_next = ends[1], fraction(after(N_S, NY))
            tx = trans_of(perm[0, at, :], after(N_K, NY))
        flow_out = carried(tx, p_here, p_next, f_here, f_next)
        total = flow_out - flow_in
        flow_in = flow_out
        beside = lambda a, e: jnp.where(end, e[x : x + 1, :], roll(a, -1, 0))
        fy = carried(
            jnp.where(end, east_t[x : x + 1, :], ty),
            p_here,
            beside(p_here, sides[1]),
            f_here,
            beside(f_here, east_f),
        )
        total = total + (fy - jnp.where(rows == 0, west_flow[x : x + 1, :], roll(fy, 1, 0)))
        fz = carried(tz, p_here, roll(p_here, -1, 1), f_here, roll(f_here, -1, 1))
        total = total + (fz - roll(fz, 1, 1))
        new_sat[at, :] = sat[at, :] - rate[at, :] * total
        p_here, f_here = p_next, f_next
        if x % 4 == 3:
            part = pl.ds((x - 3) * NY, 4 * NY)
            copy = pltpu.make_async_copy(new_sat.at[part], new_sat_out.at[part], sems.at[1 + x // 4])
            copy.start()
            copies.append(copy)
    for copy in copies:
        copy.wait()


VMEM = pl.BlockSpec(memory_space=pltpu.VMEM)
HBM = pl.BlockSpec(memory_space=pltpu.HBM)


def call(kernel, outs, scratch, flops, args, far=0, out_spec=VMEM, limit=24):
    args = [pltpu.with_memory_space_constraint(a, pltpu.HBM) for a in args[:far]] + args[far:]
    shapes = [jax.ShapeDtypeStruct(shape, jnp.float32) for shape in outs]
    size = sum(a.size * a.dtype.itemsize for a in args) + sum(4 * a.size for a in shapes)
    return pl.pallas_call(
        kernel,
        out_shape=shapes,
        in_specs=[HBM] * far + [VMEM] * (len(args) - far),
        out_specs=[out_spec] * len(shapes),
        scratch_shapes=scratch,
        compiler_params=pltpu.CompilerParams(vmem_limit_bytes=limit * 1024 * 1024),
        cost_estimate=pl.CostEstimate(flops=flops, bytes_accessed=size, transcendentals=0),
    )(*args)


def space(*shape, dtype=jnp.float32):
    return pltpu.VMEM(shape, dtype)


def swaps(n, start):
    pairs = [(i, i + 1) for i in range(start, n - 1, 2)]
    return pairs + [(j, i) for i, j in pairs]


def on_device(pressure, saturation, source, permeability, pore_volume, basis, support, matrix):
    p_in, sat_in, src_in, pore_in = (
        a.reshape(-1, L) for a in (pressure, saturation, source, pore_volume)
    )
    perm_in = permeability.reshape(3, -1, L)
    basis_in = basis.reshape(-1, L)
    support = support.transpose(0, 2, 1).reshape(NX * K, NY)
    matrix = matrix.reshape(9 * NX, NY)
    n_narrow, n_wide = lax.axis_size("narrow"), lax.axis_size("wide")
    cells, fine, middle = NX * NY, NX * NY * K, (HIGH - LOW) * NY
    out_even, out_odd, small, p, perm, sat, bs, trans = call(
        edge_kernel,
        [(N_ROWS, L), (N_ROWS, L), (SMALL * TALL, L), (cells, L), (3, cells, L), (cells, L), (fine, L), (3, cells, L)],
        [
            space(cells, L), space(fine, L, dtype=jnp.bfloat16), space(NX * K, NY, dtype=jnp.int32), space(9 * NX, NY),
            space(TALL, L), space(L, L), pltpu.SemaphoreType.DMA((13,)),
        ],
        10**7,
        [p_in, perm_in, src_in, basis_in, support, matrix, sat_in],
        far=7,
        limit=LIMIT1,
    )
    odd = lax.ppermute(out_odd, "narrow", swaps(n_narrow, 1))
    gathered = lax.all_gather(
        out_even, "narrow", axis_index_groups=[[i, i + 1] for i in range(0, n_narrow, 2)]
    )
    bs_middle, trans_middle, acc, frac, rate = call(
        middle_kernel,
        [(middle * K, L), (3, middle, L), (TALL, L), (cells, L), (cells, L)],
        [
            space(middle, L), space(middle * K, L, dtype=jnp.bfloat16), space(cells, L),
            space(L, L), pltpu.SemaphoreType.DMA((3,)),
        ],
        10**7,
        [src_in, basis_in, pore_in, p, perm, sat, small],
        far=3,
        limit=24,
    )
    sent_odd, sent_even, small = call(
        narrow_kernel,
        [(W_ROWS, L), (W_ROWS, L), (SMALL * TALL, L)],
        [space(L, L)],
        10**6,
        [gathered, odd, p, sat, perm, bs, bs_middle, small, acc],
    )
    in_odd = lax.ppermute(sent_odd, "wide", swaps(n_wide, 1))
    in_even = lax.ppermute(sent_even, "wide", swaps(n_wide, 0))
    new, new_sat = call(
        final_kernel,
        [(cells, L), (cells, L)],
        [space(cells, L), space(cells, L), space(L, L), pltpu.SemaphoreType.DMA((5,))],
        10**7,
        [
            in_odd, in_even, sent_odd, sent_even, gathered, odd, small, p, sat, perm, bs, trans,
            bs_middle, trans_middle, frac, rate,
        ],
        out_spec=HBM,
    )
    return new.reshape(pressure.shape), new_sat.reshape(pressure.shape)


def solution(mesh):
    return jax.shard_map(
        on_device,
        mesh=mesh,
        in_specs=(
            P("narrow", "wide", None),
            P("narrow", "wide", None),
            P("narrow", "wide", None),
            P(None, "narrow", "wide", None),
            P("narrow", "wide", None),
            P("narrow", "wide", None, None),
            P("narrow", "wide", None),
            P(None, "narrow", "wide"),
        ),
        out_specs=(P("narrow", "wide", None), P("narrow", "wide", None)),
        check_vma=False,
    )
```

```python
import jax
import jax.numpy as jnp
from jax import lax
from jax.experimental import pallas as pl
from jax.experimental.pallas import tpu as pltpu
from jax.sharding import PartitionSpec as P

SWEEPS = 3
OFFSETS = [(o // 3 - 1, o % 3 - 1) for o in range(9)]
OMEGA = 0.6667
DT = 0.01

NX, NY, L, K = 16, 32, 128, 4
TOP, WEST, TALL = 8, 4, 32
EDGE = 5
FIELDS = 2 + K
SUP, MAT, ACC = 0, K, K + 9
SMALL = K + 10
N_P, N_K, N_S, N_B, N_C = 0, 32, 64, 96, 224
N_SMALL = 288
N_ROWS = N_SMALL + 8 * 5
W_SAT = FIELDS * TALL
W_SMALL = W_SAT + NX
W_ROWS = W_SMALL + TALL


def roll(a, shift, axis):
    shift %= a.shape[axis]
    return pltpu.roll(a, shift, axis) if shift else a


def iota(shape, axis):
    return lax.broadcasted_iota(jnp.int32, shape, axis)


def trans_of(here, there):
    return 2.0 * here * there / (here + there)


def fraction(sat):
    rest = 1.0 - sat
    square = sat * sat
    return square / (square + 0.5 * (rest * rest))


def lane_sum(a):
    return jnp.sum(a, axis=-1, keepdims=True)


def bin_pieces(sup, pieces):
    total = None
    for dy in (-1, 0, 1):
        column = None
        for dx in (-1, 0, 1):
            code = float((dx + 1) * 3 + dy + 1)
            part = None
            for k in range(K):
                term = jnp.where(sup[k] == code, pieces[k], 0.0)
                part = term if part is None else part + term
            part = roll(part, dx, 0)
            column = part if column is None else column + part
        column = roll(column, dy, 1)
        total = column if total is None else total + column
    return total


def turned(scratch, value):
    scratch[...] = jnp.zeros((L, L), jnp.float32)
    scratch[WEST : WEST + NY, :] = value
    return scratch[...].T


def rows_residual(p, perm, src, trans, lo, hi, base):
    rows, lanes = iota((NY, L), 0), iota((NY, L), 1)

    def face(x):
        a, b = slice(x * NY, (x + 1) * NY), slice((x + 1) * NY, (x + 2) * NY)
        value = trans_of(perm[0, a, :], perm[0, b, :])
        if x >= lo:
            trans[0, (x - base) * NY : (x - base + 1) * NY, :] = value
        return value * (p[a, :] - p[b, :])

    result = []
    last = face(lo - 1) if lo > 0 else None
    for x in range(lo, hi):
        at = slice(x * NY, (x + 1) * NY)
        here, ky, kz = p[at, :], perm[1, at, :], perm[2, at, :]
        ty = jnp.where(rows < NY - 1, trans_of(ky, roll(ky, -1, 0)), 0.0)
        tz = jnp.where(lanes < L - 1, trans_of(kz, roll(kz, -1, 1)), 0.0)
        to = slice((x - base) * NY, (x - base + 1) * NY)
        trans[1, to, :] = ty
        trans[2, to, :] = tz
        fy = ty * (here - roll(here, -1, 0))
        fz = tz * (here - roll(here, -1, 1))
        total = (fy - roll(fy, 1, 0)) + (fz - roll(fz, 1, 1))
        if last is not None:
            total = total - last
        last = None
        if x < NX - 1:
            last = face(x)
            total = total + last
        result.append(src[to, :] - total)
    return result


def add_pieces(pieces, residuals, lo, bs, base):
    lanes = iota((NY, L), 1)
    for i, res in enumerate(residuals):
        x = lo + i
        for k in range(K):
            b = bs[pl.ds((x - base) * NY * K + k, NY, stride=K), :]
            pieces = jnp.where(lanes == k * TALL + TOP + x, lane_sum(b * res), pieces)
    return pieces


def split_pieces(square, pieces):
    flipped = turned(square, pieces)
    return [flipped[k * TALL : (k + 1) * TALL, :] for k in range(K)]


LIMIT1 = 24
LOW, HIGH = EDGE, NX - EDGE


def copies_of(sems, pairs):
    out = [pltpu.make_async_copy(src, dst, sems.at[i]) for i, (src, dst) in enumerate(pairs)]
    for copy in out:
        copy.start()
    return out


def edge_kernel(
    p_in, perm_in, src_in, basis_in, support_in, matrix_in, sat_in,
    out_even, out_odd, small, p, perm, sat, bs, trans,
    src, basis, support, matrix, place, square, sems,
):
    even = lax.axis_index("narrow") % 2 == 0
    top, bottom, middle = (
        pl.ds(0, (LOW + 1) * NY),
        pl.ds((HIGH - 1) * NY, (LOW + 1) * NY),
        pl.ds((LOW + 1) * NY, (HIGH - LOW - 2) * NY),
    )
    pairs = []
    for part, first in ((top, 0), (bottom, HIGH)):
        own, fine = pl.ds(first * NY, EDGE * NY), pl.ds(first * NY * K, EDGE * NY * K)
        pairs += [(p_in.at[part], p.at[part]), (perm_in.at[:, part], perm.at[:, part])]
        pairs += [(src_in.at[own], src.at[own]), (basis_in.at[fine], basis.at[fine])]
    pairs += [(support_in, support), (matrix_in, matrix), (sat_in, sat)]
    pairs += [(p_in.at[middle], p.at[middle]), (perm_in.at[:, middle], perm.at[:, middle])]
    copies = copies_of(sems, pairs)
    pieces = jnp.zeros((NY, L), jnp.float32)
    for i, first in enumerate((0, HIGH)):
        for copy in copies[4 * i : 4 * i + 3]:
            copy.wait()
        residuals = rows_residual(p, perm, src, trans, first, first + EDGE, 0)
        copies[4 * i + 3].wait()
        fine = slice(first * NY * K, (first + EDGE) * NY * K)
        bs[fine, :] = basis[fine, :].astype(jnp.float32)
        pieces = add_pieces(pieces, residuals, first, bs, 0)
    pieces = split_pieces(square, pieces)
    copies[8].wait()
    copies[9].wait()
    place[...] = jnp.zeros((TALL, L), jnp.float32)
    stack = []
    for i in range(K + 9):
        if i < MAT:
            value = support[pl.ds(i, NX, stride=K), :].astype(jnp.float32)
        else:
            value = matrix[(i - MAT) * NX : (i - MAT + 1) * NX, :]
        place[TOP : TOP + NX, 0:NY] = value
        stack.append(roll(place[...], WEST, 1))
    acc = bin_pieces(stack[:K], pieces)
    stack.append(acc)
    for i in range(SMALL):
        small[i * TALL : (i + 1) * TALL, :] = stack[i]
    copies[10].wait()
    for out, takes_last in ((out_even, even), (out_odd, jnp.logical_not(even))):
        edge = jnp.where(takes_last, NX - 1, 0)
        row = pl.multiple_of(edge * NY, NY)
        out[N_P : N_P + NY, :] = p[pl.ds(row, NY), :]
        out[N_K : N_K + NY, :] = perm[0, pl.ds(row, NY), :]
        out[N_S : N_S + NY, :] = sat[pl.ds(row, NY), :]
        for k in range(K):
            out[N_B + k * NY : N_B + (k + 1) * NY, :] = bs[pl.ds(row * K + k, NY, stride=K), :]
        start = jnp.where(takes_last, NX - EDGE, 0) * NY
        for c, col in enumerate((0, NY - 1)):
            fields = [
                p[pl.ds(start + col, EDGE, stride=NY), :],
                perm[1, pl.ds(start + col, EDGE, stride=NY), :],
            ] + [bs[pl.ds((start + col) * K + k, EDGE, stride=NY * K), :] for k in range(K)]
            for f, value in enumerate(fields):
                to = N_C + (f * 2 + c) * EDGE
                out[to : to + EDGE, :] = value
        window = [jnp.where(takes_last, s[16:24, :], s[8:16, :]) for s in stack]
        window.append(jnp.where(takes_last, acc[24:32, :], acc[0:8, :]))
        for i in range(5):
            a, b, c = window[3 * i : 3 * i + 3]
            out[N_SMALL + 8 * i : N_SMALL + 8 * i + 8, :] = a + roll(b, 40, 1) + roll(c, 80, 1)
    copies[11].wait()
    copies[12].wait()


def middle_kernel(
    src_in, basis_in, pore_in, p, perm, sat, small,
    bs, trans, acc, frac, rate,
    src, basis, pore, square, sems,
):
    own, fine = pl.ds(LOW * NY, (HIGH - LOW) * NY), pl.ds(LOW * NY * K, (HIGH - LOW) * NY * K)
    copies = copies_of(sems, [(src_in.at[own], src), (basis_in.at[fine], basis), (pore_in, pore)])
    frac[...] = fraction(sat[...])
    copies[0].wait()
    residuals = rows_residual(p, perm, src, trans, LOW, HIGH, LOW)
    copies[1].wait()
    bs[...] = basis[...].astype(jnp.float32)
    pieces = add_pieces(jnp.zeros((NY, L), jnp.float32), residuals, LOW, bs, LOW)
    sup = [small[k * TALL : (k + 1) * TALL, :] for k in range(K)]
    acc[...] = bin_pieces(sup, split_pieces(square, pieces))
    copies[2].wait()
    rate[...] = DT / pore[...]


def narrow_kernel(
    gathered, odd, p, sat, perm, bs, bs_middle, small, acc_middle, out_odd, out_even, small_out, square
):
    even = lax.axis_index("narrow") % 2 == 0
    wide_even = lax.axis_index("wide") % 2 == 0
    mate = jnp.where(even, 1, 0)
    lanes = iota((NY, L), 1)

    def before(lo, n):
        return jnp.where(even, odd[lo : lo + n, :], gathered[mate, lo : lo + n, :])

    def after(lo, n):
        return jnp.where(even, gathered[mate, lo : lo + n, :], odd[lo : lo + n, :])

    in_slot = iota((8, L), 1) < 40

    def windows(get):
        out = []
        for i in range(5):
            block = get(N_SMALL + 8 * i, 8)
            out += [jnp.where(in_slot, roll(block, -40 * j, 1), 0.0) for j in range(3)]
        return out

    top, bottom = windows(before), windows(after)
    none = jnp.zeros((8, L), jnp.float32)
    stack = []
    for i in range(SMALL):
        own = small[i * TALL : (i + 1) * TALL, :]
        if i < ACC:
            own = own[8:24, :]
            stack.append(jnp.concatenate([top[i], own, bottom[i]], axis=0))
        else:
            stack.append(own + jnp.concatenate([top[i], top[i + 1], bottom[i + 1], bottom[i]], axis=0))
    pieces = jnp.zeros((NY, L), jnp.float32)
    for x, other_x, get in ((0, -1, before), (NX - 1, NX, after)):
        at = x * NY
        flux = trans_of(perm[0, at : at + NY, :], get(N_K, NY)) * (p[at : at + NY, :] - get(N_P, NY))
        for k in range(K):
            mine = lane_sum(bs[pl.ds(at * K + k, NY, stride=K), :] * -flux)
            pieces = jnp.where(lanes == k * TALL + TOP + x, mine, pieces)
            other = lane_sum(get(N_B + k * NY, NY) * flux)
            pieces = jnp.where(lanes == k * TALL + TOP + other_x, other, pieces)
    stack[ACC] = stack[ACC] + acc_middle[...] + bin_pieces(stack[:K], split_pieces(square, pieces))
    for i in range(SMALL):
        small_out[i * TALL : (i + 1) * TALL, :] = stack[i]
    slot = iota((TALL, L), 1) // 8
    first = jnp.zeros((TALL, L), jnp.float32)
    last = jnp.zeros((TALL, L), jnp.float32)
    for i in range(SMALL):
        first = jnp.where(slot == i, roll(stack[i], 8 * i, 1), first)
        last = jnp.where(slot == i, roll(stack[i], 8 * i - 32, 1), last)
    blank = jnp.zeros((8, L), jnp.float32)
    for out, takes_last in ((out_even, wide_even), (out_odd, jnp.logical_not(wide_even))):
        col = jnp.where(takes_last, NY - 1, 0)
        for f in range(FIELDS):
            base = f * TALL
            lo = N_C + f * 2 * EDGE
            out[base : base + 8, :] = blank
            out[base + 24 : base + 32, :] = blank
            out[base + 3 : base + 8, :] = jnp.where(takes_last, before(lo + EDGE, EDGE), before(lo, EDGE))
            if f < 2:
                field = p[pl.ds(col, NX, stride=NY), :] if f == 0 else perm[1, pl.ds(col, NX, stride=NY), :]
                out[base + TOP : base + TOP + NX, :] = field
            else:
                at = col * K + f - 2
                for ref, x, start, n in (
                    (bs, 0, 0, LOW), (bs_middle, LOW, 0, HIGH - LOW), (bs, HIGH, HIGH, NX - HIGH)
                ):
                    column = ref[pl.ds(start * NY * K + at, n, stride=NY * K), :]
                    out[base + TOP + x : base + TOP + x + n, :] = column
            out[base + 24 : base + 29, :] = jnp.where(takes_last, after(lo + EDGE, EDGE), after(lo, EDGE))
        out[W_SAT : W_SAT + NX, :] = sat[pl.ds(col, NX, stride=NY), :]
        out[W_SMALL : W_SMALL + TALL, :] = jnp.where(takes_last, last, first)


def final_kernel(
    in_odd, in_even, sent_odd, sent_even, gathered, odd, small, p, sat, perm, bs, trans, bs_middle, trans_middle, frac, rate,
    new_out, new_sat_out,
    new, new_sat, square, sems,
):
    even = lax.axis_index("narrow") % 2 == 0
    wide_even = lax.axis_index("wide") % 2 == 0
    mate = jnp.where(even, 1, 0)

    def before(lo, n):
        return jnp.where(even, odd[lo : lo + n, :], gathered[mate, lo : lo + n, :])

    def after(lo, n):
        return jnp.where(even, gathered[mate, lo : lo + n, :], odd[lo : lo + n, :])

    place = lax.axis_index("wide")
    inside = jnp.logical_and(place > 0, place < lax.axis_size("wide") - 1)
    odd_mate = jnp.where(wide_even, 0, 1)

    def odd_side(lo, n):
        return jnp.where(inside, in_odd[odd_mate, lo : lo + n, :], 0.0)

    def left(lo, n):
        return jnp.where(wide_even, odd_side(lo, n), in_even[lo : lo + n, :])

    def right(lo, n):
        return jnp.where(wide_even, in_even[lo : lo + n, :], odd_side(lo, n))

    def first(lo, n):
        return jnp.where(wide_even, sent_odd[lo : lo + n, :], sent_even[lo : lo + n, :])

    def last(lo, n):
        return jnp.where(wide_even, sent_even[lo : lo + n, :], sent_odd[lo : lo + n, :])

    lane = iota((TALL, L), 1)
    from_left, from_right = left(W_SMALL, TALL), right(W_SMALL, TALL)
    stack = []
    for i in range(SMALL):
        own = small[i * TALL : (i + 1) * TALL, :]
        own = own + jnp.where(lane < 8, roll(from_left, -8 * i, 1), 0.0)
        own = own + jnp.where(lane // 8 == 4, roll(from_right, 32 - 8 * i, 1), 0.0)
        stack.append(own)
    sup, mat = stack[:K], stack[MAT : MAT + 9]
    pieces = [jnp.zeros((TALL, L), jnp.float32)] * K
    for mine, other, y, other_y in ((first, left, 0, -1), (last, right, NY - 1, NY)):
        k_here, k_there = mine(TALL, TALL), other(TALL, TALL)
        total = k_here + k_there
        flux = (2.0 * k_here * k_there / jnp.where(total > 0, total, 1.0)) * (mine(0, TALL) - other(0, TALL))
        for k in range(K):
            lo = (2 + k) * TALL
            here = lane_sum(mine(lo, TALL) * -flux)
            there = lane_sum(other(lo, TALL) * flux)
            pieces[k] = jnp.where(lane == WEST + y, here, pieces[k])
            pieces[k] = jnp.where(lane == WEST + other_y, there, pieces[k])
    res = stack[ACC] + bin_pieces(sup, pieces)
    diag = mat[4]
    scale = jnp.where(diag > 0, OMEGA / jnp.where(diag > 0, diag, 1.0), 0.0)

    def moved(coarse):
        sides = {dy: roll(coarse, -dy, 1) for dy in (-1, 0, 1)}
        return [roll(sides[dy], -dx, 0) for dx, dy in OFFSETS]

    coarse = scale * res
    for _ in range(SWEEPS - 1):
        rest = res
        for o, value in enumerate(moved(coarse)):
            rest = rest - mat[o] * value
        coarse = coarse + scale * rest
    shifts = moved(coarse)
    picked = []
    for k in range(K):
        total = jnp.zeros((TALL, L), jnp.float32)
        for o in range(9):
            total = jnp.where(sup[k] == float(o), shifts[o], total)
        picked.append(total)
    for k in range(K):
        square[k * TALL : (k + 1) * TALL, :] = roll(picked[k], -WEST, 1)
    weights = square[...].T[0:NY, :]

    def weight(k, x):
        at = k * TALL + TOP + x
        return weights[:, at : at + 1]

    for x in range(NX):
        at = slice(x * NY, (x + 1) * NY)
        total = p[at, :]
        ref, base = (bs_middle, LOW) if LOW <= x < HIGH else (bs, 0)
        for k in range(K):
            total = total + ref[pl.ds((x - base) * NY * K + k, NY, stride=K), :] * weight(k, x)
        new[at, :] = total
    copies = copies_of(sems, [(new, new_out)])
    ends = []
    for get, x in ((before, -1), (after, NX)):
        total = get(N_P, NY)
        for k in range(K):
            total = total + get(N_B + k * NY, NY) * weight(k, x)
        ends.append(total)
    sides = []
    for get, y in ((left, -1), (right, NY)):
        total = get(TOP, NX)
        for k in range(K):
            column = picked[k][TOP : TOP + NX, WEST + y : WEST + y + 1]
            total = total + get((2 + k) * TALL + TOP, NX) * column
        sides.append(total)

    def carried(value, here, there, f_here, f_there):
        flux = value * (here - there)
        return flux * jnp.where(flux > 0, f_here, f_there)

    west_f, east_f = fraction(left(W_SAT, NX)), fraction(right(W_SAT, NX))
    east_t = trans_of(perm[1, pl.ds(NY - 1, NX, stride=NY), :], right(TALL + TOP, NX))
    west_flow = carried(
        trans_of(perm[1, pl.ds(0, NX, stride=NY), :], left(TALL + TOP, NX)),
        sides[0],
        new[pl.ds(0, NX, stride=NY), :],
        west_f,
        frac[pl.ds(0, NX, stride=NY), :],
    )
    rows = iota((NY, L), 0)
    end = rows == NY - 1
    p_here, f_here = new[0:NY, :], frac[0:NY, :]
    flow_in = carried(
        trans_of(before(N_K, NY), perm[0, 0:NY, :]), ends[0], p_here, fraction(before(N_S, NY)), f_here
    )
    for x in range(NX):
        at = slice(x * NY, (x + 1) * NY)
        ref, base = (trans_middle, LOW) if LOW <= x < HIGH else (trans, 0)
        tx, ty, tz = (ref[c, (x - base) * NY : (x - base + 1) * NY, :] for c in range(3))
        if x < NX - 1:
            nxt = slice((x + 1) * NY, (x + 2) * NY)
            p_next, f_next = new[nxt, :], frac[nxt, :]
        else:
            p_next, f_next = ends[1], fraction(after(N_S, NY))
            tx = trans_of(perm[0, at, :], after(N_K, NY))
        flow_out = carried(tx, p_here, p_next, f_here, f_next)
        total = flow_out - flow_in
        flow_in = flow_out
        beside = lambda a, e: jnp.where(end, e[x : x + 1, :], roll(a, -1, 0))
        fy = carried(
            jnp.where(end, east_t[x : x + 1, :], ty),
            p_here,
            beside(p_here, sides[1]),
            f_here,
            beside(f_here, east_f),
        )
        total = total + (fy - jnp.where(rows == 0, west_flow[x : x + 1, :], roll(fy, 1, 0)))
        fz = carried(tz, p_here, roll(p_here, -1, 1), f_here, roll(f_here, -1, 1))
        total = total + (fz - roll(fz, 1, 1))
        new_sat[at, :] = sat[at, :] - rate[at, :] * total
        p_here, f_here = p_next, f_next
        if x % 4 == 3:
            part = pl.ds((x - 3) * NY, 4 * NY)
            copy = pltpu.make_async_copy(new_sat.at[part], new_sat_out.at[part], sems.at[1 + x // 4])
            copy.start()
            copies.append(copy)
    for copy in copies:
        copy.wait()


VMEM = pl.BlockSpec(memory_space=pltpu.VMEM)
HBM = pl.BlockSpec(memory_space=pltpu.HBM)


def call(kernel, outs, scratch, flops, args, far=0, out_spec=VMEM, limit=24):
    args = [pltpu.with_memory_space_constraint(a, pltpu.HBM) for a in args[:far]] + args[far:]
    shapes = [jax.ShapeDtypeStruct(shape, jnp.float32) for shape in outs]
    size = sum(a.size * a.dtype.itemsize for a in args) + sum(4 * a.size for a in shapes)
    return pl.pallas_call(
        kernel,
        out_shape=shapes,
        in_specs=[HBM] * far + [VMEM] * (len(args) - far),
        out_specs=[out_spec] * len(shapes),
        scratch_shapes=scratch,
        compiler_params=pltpu.CompilerParams(vmem_limit_bytes=limit * 1024 * 1024),
        cost_estimate=pl.CostEstimate(flops=flops, bytes_accessed=size, transcendentals=0),
    )(*args)


def space(*shape, dtype=jnp.float32):
    return pltpu.VMEM(shape, dtype)


def swaps(n, start):
    pairs = [(i, i + 1) for i in range(start, n - 1, 2)]
    return pairs + [(j, i) for i, j in pairs]


def on_device(pressure, saturation, source, permeability, pore_volume, basis, support, matrix):
    p_in, sat_in, src_in, pore_in = (
        a.reshape(-1, L) for a in (pressure, saturation, source, pore_volume)
    )
    perm_in = permeability.reshape(3, -1, L)
    basis_in = basis.reshape(-1, L)
    support = support.transpose(0, 2, 1).reshape(NX * K, NY)
    matrix = matrix.reshape(9 * NX, NY)
    n_narrow, n_wide = lax.axis_size("narrow"), lax.axis_size("wide")
    cells, fine, middle = NX * NY, NX * NY * K, (HIGH - LOW) * NY
    out_even, out_odd, small, p, perm, sat, bs, trans = call(
        edge_kernel,
        [(N_ROWS, L), (N_ROWS, L), (SMALL * TALL, L), (cells, L), (3, cells, L), (cells, L), (fine, L), (3, cells, L)],
        [
            space(cells, L), space(fine, L, dtype=jnp.bfloat16), space(NX * K, NY, dtype=jnp.int32), space(9 * NX, NY),
            space(TALL, L), space(L, L), pltpu.SemaphoreType.DMA((13,)),
        ],
        10**7,
        [p_in, perm_in, src_in, basis_in, support, matrix, sat_in],
        far=7,
        limit=LIMIT1,
    )
    odd = lax.ppermute(out_odd, "narrow", swaps(n_narrow, 1))
    gathered = lax.all_gather(
        out_even, "narrow", axis_index_groups=[[i, i + 1] for i in range(0, n_narrow, 2)]
    )
    bs_middle, trans_middle, acc, frac, rate = call(
        middle_kernel,
        [(middle * K, L), (3, middle, L), (TALL, L), (cells, L), (cells, L)],
        [
            space(middle, L), space(middle * K, L, dtype=jnp.bfloat16), space(cells, L),
            space(L, L), pltpu.SemaphoreType.DMA((3,)),
        ],
        10**7,
        [src_in, basis_in, pore_in, p, perm, sat, small],
        far=3,
        limit=24,
    )
    sent_odd, sent_even, small = call(
        narrow_kernel,
        [(W_ROWS, L), (W_ROWS, L), (SMALL * TALL, L)],
        [space(L, L)],
        10**6,
        [gathered, odd, p, sat, perm, bs, bs_middle, small, acc],
    )
    in_even = lax.ppermute(sent_even, "wide", swaps(n_wide, 0))
    in_odd = lax.all_gather(
        sent_odd, "wide", axis_index_groups=[[i, (i + 1) % n_wide] for i in range(1, n_wide, 2)]
    )
    new, new_sat = call(
        final_kernel,
        [(cells, L), (cells, L)],
        [space(cells, L), space(cells, L), space(L, L), pltpu.SemaphoreType.DMA((5,))],
        10**7,
        [
            in_odd, in_even, sent_odd, sent_even, gathered, odd, small, p, sat, perm, bs, trans,
            bs_middle, trans_middle, frac, rate,
        ],
        out_spec=HBM,
    )
    return new.reshape(pressure.shape), new_sat.reshape(pressure.shape)


def solution(mesh):
    return jax.shard_map(
        on_device,
        mesh=mesh,
        in_specs=(
            P("narrow", "wide", None),
            P("narrow", "wide", None),
            P("narrow", "wide", None),
            P(None, "narrow", "wide", None),
            P("narrow", "wide", None),
            P("narrow", "wide", None, None),
            P("narrow", "wide", None),
            P(None, "narrow", "wide"),
        ),
        out_specs=(P("narrow", "wide", None), P("narrow", "wide", None)),
        check_vma=False,
    )
```

```python
import jax
import jax.numpy as jnp
from jax import lax
from jax.experimental import pallas as pl
from jax.experimental.pallas import tpu as pltpu
from jax.sharding import PartitionSpec as P

SWEEPS = 3
OFFSETS = [(o // 3 - 1, o % 3 - 1) for o in range(9)]
OMEGA = 0.6667
DT = 0.01

NX, NY, L, K = 16, 32, 128, 4
TOP, WEST, TALL = 8, 4, 32
EDGE = 5
FIELDS = 2 + K
SUP, MAT, ACC = 0, K, K + 9
SMALL = K + 10
N_P, N_K, N_S, N_B, N_C = 0, 32, 64, 96, 224
N_SMALL = 288
N_ROWS = N_SMALL + 8 * 5
COLUMN = NX + 2 * EDGE
MARGIN = TOP - EDGE
W_SAT = 0
W_FIELD = NX
W_SMALL = W_FIELD + FIELDS * COLUMN
W_ROWS = W_SMALL + COLUMN + 10


def roll(a, shift, axis):
    shift %= a.shape[axis]
    return pltpu.roll(a, shift, axis) if shift else a


def iota(shape, axis):
    return lax.broadcasted_iota(jnp.int32, shape, axis)


def trans_of(here, there):
    return 2.0 * here * there / (here + there)


def fraction(sat):
    rest = 1.0 - sat
    square = sat * sat
    return square / (square + 0.5 * (rest * rest))


def lane_sum(a):
    return jnp.sum(a, axis=-1, keepdims=True)


def halves(a):
    high = a.astype(jnp.bfloat16)
    return high, (a - high.astype(jnp.float32)).astype(jnp.bfloat16)


def bin_pieces(sup, pieces):
    total = None
    for dy in (-1, 0, 1):
        column = None
        for dx in (-1, 0, 1):
            code = float((dx + 1) * 3 + dy + 1)
            part = None
            for k in range(K):
                term = jnp.where(sup[k] == code, pieces[k], 0.0)
                part = term if part is None else part + term
            part = roll(part, dx, 0)
            column = part if column is None else column + part
        column = roll(column, dy, 1)
        total = column if total is None else total + column
    return total


def turned(scratch, value):
    scratch[...] = jnp.zeros((L, L), jnp.float32)
    scratch[WEST : WEST + NY, :] = value
    return scratch[...].T


def rows_residual(p, perm, src, trans, lo, hi, base):
    rows, lanes = iota((NY, L), 0), iota((NY, L), 1)

    def face(x):
        a, b = slice((x - base) * NY, (x - base + 1) * NY), slice((x - base + 1) * NY, (x - base + 2) * NY)
        value = trans_of(perm[0, a, :], perm[0, b, :])
        trans[0, a, :] = value
        return value * (p[a, :] - p[b, :])

    result = []
    last = face(lo - 1) if lo > 0 else None
    for x in range(lo, hi):
        at = slice((x - base) * NY, (x - base + 1) * NY)
        here, ky, kz = p[at, :], perm[1, at, :], perm[2, at, :]
        ty = jnp.where(rows < NY - 1, trans_of(ky, roll(ky, -1, 0)), 0.0)
        tz = jnp.where(lanes < L - 1, trans_of(kz, roll(kz, -1, 1)), 0.0)
        trans[1, at, :] = ty
        trans[2, at, :] = tz
        fy = ty * (here - roll(here, -1, 0))
        fz = tz * (here - roll(here, -1, 1))
        total = (fy - roll(fy, 1, 0)) + (fz - roll(fz, 1, 1))
        if last is not None:
            total = total - last
        last = None
        if x < NX - 1:
            last = face(x)
            total = total + last
        result.append(src[at, :] - total)
    return result


def add_pieces(pieces, residuals, lo, mixed, bs, base):
    lanes = iota((NY, L), 1)
    for i, res in enumerate(residuals):
        x = lo + i
        for k in range(K):
            b = mixed[pl.ds((x - base) * NY * K + k, NY, stride=K), :]
            bs[k, (x - base) * NY : (x - base + 1) * NY, :] = b
            pieces = jnp.where(lanes == k * TALL + TOP + x, lane_sum(b * res), pieces)
    return pieces


def split_pieces(square, pieces):
    flipped = turned(square, pieces)
    return [flipped[k * TALL : (k + 1) * TALL, :] for k in range(K)]


LOW, HIGH = EDGE, NX - EDGE


def copies_of(sems, pairs):
    out = [pltpu.make_async_copy(src, dst, sems.at[i]) for i, (src, dst) in enumerate(pairs)]
    for copy in out:
        copy.start()
    return out


def edge_kernel(
    p_in, perm_in, src_in, basis_in, support_in, matrix_in, sat_in,
    out_even, out_odd, small, p, perm, bs, trans, basis,
    src, mixed, support, matrix, place, square, sems,
):
    even = lax.axis_index("narrow") % 2 == 0
    rows_even = pl.ds(pl.multiple_of(jnp.where(even, NX - 1, 0) * NY, NY), NY)
    rows_odd = pl.ds(pl.multiple_of(jnp.where(even, 0, NX - 1) * NY, NY), NY)
    pairs = []
    for near, first in ((0, 0), (HIGH - 1, HIGH)):
        part = pl.ds(near * NY, (EDGE + 1) * NY)
        own, fine = pl.ds(first * NY, EDGE * NY), pl.ds(first * NY * K, EDGE * NY * K)
        pairs += [(p_in.at[part], p.at[part]), (perm_in.at[:, part], perm.at[:, part])]
        pairs += [(src_in.at[own], src.at[own]), (basis_in.at[fine], basis.at[fine])]
    pairs += [(support_in, support), (matrix_in, matrix)]
    pairs += [(sat_in.at[rows_even], out_even.at[pl.ds(N_S, NY)])]
    pairs += [(sat_in.at[rows_odd], out_odd.at[pl.ds(N_S, NY)])]
    copies = copies_of(sems, pairs)
    pieces = jnp.zeros((NY, L), jnp.float32)
    for i, first in enumerate((0, HIGH)):
        for copy in copies[4 * i : 4 * i + 3]:
            copy.wait()
        residuals = rows_residual(p, perm, src, trans, first, first + EDGE, 0)
        copies[4 * i + 3].wait()
        fine = slice(first * NY * K, (first + EDGE) * NY * K)
        mixed[fine, :] = basis[fine, :].astype(jnp.float32)
        pieces = add_pieces(pieces, residuals, first, mixed, bs, 0)
    pieces = split_pieces(square, pieces)
    copies[8].wait()
    copies[9].wait()
    place[...] = jnp.zeros((TALL, L), jnp.float32)
    stack = []
    for i in range(K + 9):
        if i < MAT:
            value = support[pl.ds(i, NX, stride=K), :].astype(jnp.float32)
        else:
            value = matrix[(i - MAT) * NX : (i - MAT + 1) * NX, :]
        place[TOP : TOP + NX, 0:NY] = value
        stack.append(roll(place[...], WEST, 1))
    acc = bin_pieces(stack[:K], pieces)
    stack.append(acc)
    for i in range(SMALL):
        small[i * TALL : (i + 1) * TALL, :] = stack[i]
    for out, takes_last in ((out_even, even), (out_odd, jnp.logical_not(even))):
        edge = jnp.where(takes_last, NX - 1, 0)
        row = pl.multiple_of(edge * NY, NY)
        out[N_P : N_P + NY, :] = p[pl.ds(row, NY), :]
        out[N_K : N_K + NY, :] = perm[0, pl.ds(row, NY), :]
        for k in range(K):
            out[N_B + k * NY : N_B + (k + 1) * NY, :] = bs[k, pl.ds(row, NY), :]
        start = jnp.where(takes_last, NX - EDGE, 0) * NY
        for c, col in enumerate((0, NY - 1)):
            fields = [
                p[pl.ds(start + col, EDGE, stride=NY), :],
                perm[1, pl.ds(start + col, EDGE, stride=NY), :],
            ] + [bs[k, pl.ds(start + col, EDGE, stride=NY), :] for k in range(K)]
            for f, value in enumerate(fields):
                to = N_C + (f * 2 + c) * EDGE
                out[to : to + EDGE, :] = value
        window = [jnp.where(takes_last, s[16:24, :], s[8:16, :]) for s in stack]
        window.append(jnp.where(takes_last, acc[24:32, :], acc[0:8, :]))
        for i in range(5):
            a, b, c = window[3 * i : 3 * i + 3]
            out[N_SMALL + 8 * i : N_SMALL + 8 * i + 8, :] = a + roll(b, 40, 1) + roll(c, 80, 1)
    copies[10].wait()
    copies[11].wait()


def middle_kernel(
    p_in, perm_in, src_in, basis_in, sat_in, pore_in, small,
    p, perm, bs, trans, acc, sat, frac, rate, basis,
    src, mixed, pore, square, sems,
):
    near = pl.ds((LOW - 1) * NY, (HIGH - LOW + 2) * NY)
    own, fine = pl.ds(LOW * NY, (HIGH - LOW) * NY), pl.ds(LOW * NY * K, (HIGH - LOW) * NY * K)
    inner = pl.ds(NY, (HIGH - LOW) * NY)
    copies = copies_of(
        sems,
        [
            (p_in.at[near], p), (perm_in.at[:, near], perm), (src_in.at[own], src.at[inner]),
            (basis_in.at[fine], basis), (sat_in, sat), (pore_in, pore),
        ],
    )
    for copy in copies[:3]:
        copy.wait()
    residuals = rows_residual(p, perm, src, trans, LOW, HIGH, LOW - 1)
    copies[3].wait()
    mixed[...] = basis[...].astype(jnp.float32)
    pieces = add_pieces(jnp.zeros((NY, L), jnp.float32), residuals, LOW, mixed, bs, LOW)
    sup = [small[k * TALL : (k + 1) * TALL, :] for k in range(K)]
    acc[...] = bin_pieces(sup, split_pieces(square, pieces))
    copies[4].wait()
    frac[...] = fraction(sat[...])
    copies[5].wait()
    rate[...] = DT / pore[...]


def narrow_kernel(
    gathered, odd, p, perm, bs, p_middle, perm_middle, bs_middle, sat, small, acc_middle, out_odd, out_even, small_out, square
):
    even = lax.axis_index("narrow") % 2 == 0
    wide_even = lax.axis_index("wide") % 2 == 0
    mate = jnp.where(even, 1, 0)
    lanes = iota((NY, L), 1)

    def before(lo, n):
        return jnp.where(even, odd[lo : lo + n, :], gathered[mate, lo : lo + n, :])

    def after(lo, n):
        return jnp.where(even, gathered[mate, lo : lo + n, :], odd[lo : lo + n, :])

    in_slot = iota((8, L), 1) < 40

    def windows(get):
        out = []
        for i in range(5):
            block = get(N_SMALL + 8 * i, 8)
            out += [jnp.where(in_slot, roll(block, -40 * j, 1), 0.0) for j in range(3)]
        return out

    top, bottom = windows(before), windows(after)
    none = jnp.zeros((8, L), jnp.float32)
    stack = []
    for i in range(SMALL):
        own = small[i * TALL : (i + 1) * TALL, :]
        if i < ACC:
            own = own[8:24, :]
            stack.append(jnp.concatenate([top[i], own, bottom[i]], axis=0))
        else:
            stack.append(own + jnp.concatenate([top[i], top[i + 1], bottom[i + 1], bottom[i]], axis=0))
    pieces = jnp.zeros((NY, L), jnp.float32)
    for x, other_x, get in ((0, -1, before), (NX - 1, NX, after)):
        at = x * NY
        flux = trans_of(perm[0, at : at + NY, :], get(N_K, NY)) * (p[at : at + NY, :] - get(N_P, NY))
        for k in range(K):
            mine = lane_sum(bs[k, at : at + NY, :] * -flux)
            pieces = jnp.where(lanes == k * TALL + TOP + x, mine, pieces)
            other = lane_sum(get(N_B + k * NY, NY) * flux)
            pieces = jnp.where(lanes == k * TALL + TOP + other_x, other, pieces)
    stack[ACC] = stack[ACC] + acc_middle[...] + bin_pieces(stack[:K], split_pieces(square, pieces))
    for i in range(SMALL):
        small_out[i * TALL : (i + 1) * TALL, :] = stack[i]
    slot = iota((TALL, L), 1) // 8
    first = jnp.zeros((TALL, L), jnp.float32)
    last = jnp.zeros((TALL, L), jnp.float32)
    for i in range(SMALL):
        first = jnp.where(slot == i, roll(stack[i], 8 * i, 1), first)
        last = jnp.where(slot == i, roll(stack[i], 8 * i - 32, 1), last)
    for out, takes_last in ((out_even, wide_even), (out_odd, jnp.logical_not(wide_even))):
        col = jnp.where(takes_last, NY - 1, 0)
        for f in range(FIELDS):
            base = W_FIELD + f * COLUMN
            lo = N_C + f * 2 * EDGE
            out[base : base + EDGE, :] = jnp.where(takes_last, before(lo + EDGE, EDGE), before(lo, EDGE))
            base += EDGE
            for middle, x, n in ((False, 0, LOW), (True, LOW, HIGH - LOW), (False, HIGH, NX - HIGH)):
                rows = pl.ds((x - LOW) * NY + col if middle else x * NY + col, n, stride=NY)
                after_first = pl.ds((x - LOW + 1) * NY + col if middle else x * NY + col, n, stride=NY)
                if f == 0:
                    column = (p_middle if middle else p)[after_first, :]
                elif f == 1:
                    column = (perm_middle if middle else perm)[1, after_first, :]
                else:
                    column = (bs_middle if middle else bs)[f - 2, rows, :]
                out[base + x : base + x + n, :] = column
            base += NX
            out[base : base + EDGE, :] = jnp.where(takes_last, after(lo + EDGE, EDGE), after(lo, EDGE))
        out[W_SAT : W_SAT + NX, :] = sat[pl.ds(col, NX, stride=NY), :]
        out[W_SMALL : W_SMALL + COLUMN, :] = jnp.where(takes_last, last, first)[MARGIN : MARGIN + COLUMN, :]
        out[W_SMALL + COLUMN : W_ROWS, :] = jnp.zeros((W_ROWS - W_SMALL - COLUMN, L), jnp.float32)


def final_kernel(
    in_odd, in_even, sent_odd, sent_even, gathered, odd, small, p, perm, basis, trans,
    p_middle, basis_middle, trans_middle, sat, frac, rate,
    new_out, new_sat_out,
    new, new_sat, square, sems,
):
    even = lax.axis_index("narrow") % 2 == 0
    wide_even = lax.axis_index("wide") % 2 == 0
    mate = jnp.where(even, 1, 0)

    def before(lo, n):
        return jnp.where(even, odd[lo : lo + n, :], gathered[mate, lo : lo + n, :])

    def after(lo, n):
        return jnp.where(even, gathered[mate, lo : lo + n, :], odd[lo : lo + n, :])

    def left(lo, n):
        return jnp.where(wide_even, in_odd[lo : lo + n, :], in_even[lo : lo + n, :])

    def right(lo, n):
        return jnp.where(wide_even, in_even[lo : lo + n, :], in_odd[lo : lo + n, :])

    def first(lo, n):
        return jnp.where(wide_even, sent_odd[lo : lo + n, :], sent_even[lo : lo + n, :])

    def last(lo, n):
        return jnp.where(wide_even, sent_even[lo : lo + n, :], sent_odd[lo : lo + n, :])

    lane = iota((TALL, L), 1)
    row = iota((TALL, L), 0)
    sent = jnp.logical_and(row >= MARGIN, row < MARGIN + COLUMN)

    def column_of(get, f):
        return get(W_FIELD + f * COLUMN - MARGIN, TALL)

    def own_rows(get, f):
        return get(W_FIELD + f * COLUMN + EDGE, NX)

    from_left, from_right = (jnp.where(sent, column_of(get, FIELDS), 0.0) for get in (left, right))
    stack = []
    for i in range(SMALL):
        own = small[i * TALL : (i + 1) * TALL, :]
        own = own + jnp.where(lane < 8, roll(from_left, -8 * i, 1), 0.0)
        own = own + jnp.where(lane // 8 == 4, roll(from_right, 32 - 8 * i, 1), 0.0)
        stack.append(own)
    sup, mat = stack[:K], stack[MAT : MAT + 9]
    pieces = [jnp.zeros((TALL, L), jnp.float32)] * K
    for mine, other, y, other_y in ((first, left, 0, -1), (last, right, NY - 1, NY)):
        k_here, k_there = column_of(mine, 1), column_of(other, 1)
        total = k_here + k_there
        flux = (2.0 * k_here * k_there / jnp.where(total > 0, total, 1.0)) * (
            column_of(mine, 0) - column_of(other, 0)
        )
        for k in range(K):
            here = lane_sum(column_of(mine, 2 + k) * -flux)
            there = lane_sum(column_of(other, 2 + k) * flux)
            pieces[k] = jnp.where(lane == WEST + y, here, pieces[k])
            pieces[k] = jnp.where(lane == WEST + other_y, there, pieces[k])
    res = stack[ACC] + bin_pieces(sup, pieces)
    diag = mat[4]
    scale = jnp.where(diag > 0, OMEGA / jnp.where(diag > 0, diag, 1.0), 0.0)

    def moved(coarse):
        sides = {dy: roll(coarse, -dy, 1) for dy in (-1, 0, 1)}
        return [roll(sides[dy], -dx, 0) for dx, dy in OFFSETS]

    coarse = scale * res
    for _ in range(SWEEPS - 1):
        rest = res
        for o, value in enumerate(moved(coarse)):
            rest = rest - mat[o] * value
        coarse = coarse + scale * rest
    shifts = moved(coarse)
    picked = []
    for k in range(K):
        total = jnp.zeros((TALL, L), jnp.float32)
        for o in range(9):
            total = jnp.where(sup[k] == float(o), shifts[o], total)
        picked.append(total)
    spread = jnp.zeros((TALL, L), jnp.float32)
    for k in range(K):
        spread = jnp.where(lane // NY == k, roll(picked[k], k * NY - WEST, 1), spread)
    spread = jnp.concatenate(halves(spread), axis=0)
    source = iota((L, L), 0)
    reorder = iota((L, L), 1) == (source % NY) * K + source // NY
    square[0 : 2 * TALL, :] = jnp.dot(
        spread, reorder.astype(jnp.bfloat16), preferred_element_type=jnp.float32
    )
    square[2 * TALL :, :] = spread.astype(jnp.float32)
    rows, lanes = iota((NY, L), 0), iota((NY, L), 1)

    def prolonged(values, start, x, mine):
        parts = []
        for at in (start, start + TALL):
            parts.append(jnp.where(mine, square[at + TOP + x : at + TOP + x + 1, :], 0.0))
        weights = jnp.concatenate(parts, axis=0).astype(jnp.bfloat16)
        both = jnp.dot(weights, values, preferred_element_type=jnp.float32)
        return both[:NY, :] + both[NY:, :]

    own = lanes // K == rows
    for x in range(NX):
        at = slice(x * NY, (x + 1) * NY)
        inner = LOW <= x < HIGH
        before_x = p_middle[(x - LOW + 1) * NY : (x - LOW + 2) * NY, :] if inner else p[at, :]
        ref, base = (basis_middle, LOW) if inner else (basis, 0)
        values = ref[(x - base) * NY * K : (x - base + 1) * NY * K, :]
        new[at, :] = before_x + prolonged(values, 0, x, own)
    copies = copies_of(sems, [(new, new_out)])
    ends = []
    own = lanes % NY == rows
    for get, x in ((before, -1), (after, NX)):
        values = get(N_B, K * NY).astype(jnp.bfloat16)
        ends.append(get(N_P, NY) + prolonged(values, 2 * TALL, x, own))
    sides = []
    for get, y in ((left, -1), (right, NY)):
        total = own_rows(get, 0)
        for k in range(K):
            column = picked[k][TOP : TOP + NX, WEST + y : WEST + y + 1]
            total = total + own_rows(get, 2 + k) * column
        sides.append(total)

    def carried(value, here, there, f_here, f_there):
        flux = value * (here - there)
        return flux * jnp.where(flux > 0, f_here, f_there)

    west_f, east_f = fraction(left(W_SAT, NX)), fraction(right(W_SAT, NX))
    east_t = trans_of(own_rows(last, 1), own_rows(right, 1))
    west_flow = carried(
        trans_of(own_rows(first, 1), own_rows(left, 1)),
        sides[0],
        new[pl.ds(0, NX, stride=NY), :],
        west_f,
        frac[pl.ds(0, NX, stride=NY), :],
    )
    end = rows == NY - 1
    p_here, f_here = new[0:NY, :], frac[0:NY, :]
    flow_in = carried(
        trans_of(before(N_K, NY), perm[0, 0:NY, :]), ends[0], p_here, fraction(before(N_S, NY)), f_here
    )
    for x in range(NX):
        at = slice(x * NY, (x + 1) * NY)
        ref, base = (trans_middle, LOW - 1) if LOW <= x < HIGH else (trans, 0)
        tx, ty, tz = (ref[c, (x - base) * NY : (x - base + 1) * NY, :] for c in range(3))
        if x < NX - 1:
            nxt = slice((x + 1) * NY, (x + 2) * NY)
            p_next, f_next = new[nxt, :], frac[nxt, :]
        else:
            p_next, f_next = ends[1], fraction(after(N_S, NY))
            tx = trans_of(perm[0, at, :], after(N_K, NY))
        flow_out = carried(tx, p_here, p_next, f_here, f_next)
        total = flow_out - flow_in
        flow_in = flow_out
        beside = lambda a, e: jnp.where(end, e[x : x + 1, :], roll(a, -1, 0))
        fy = carried(
            jnp.where(end, east_t[x : x + 1, :], ty),
            p_here,
            beside(p_here, sides[1]),
            f_here,
            beside(f_here, east_f),
        )
        total = total + (fy - jnp.where(rows == 0, west_flow[x : x + 1, :], roll(fy, 1, 0)))
        fz = carried(tz, p_here, roll(p_here, -1, 1), f_here, roll(f_here, -1, 1))
        total = total + (fz - roll(fz, 1, 1))
        new_sat[at, :] = sat[at, :] - rate[at, :] * total
        p_here, f_here = p_next, f_next
        if x % 4 == 3:
            part = pl.ds((x - 3) * NY, 4 * NY)
            copy = pltpu.make_async_copy(new_sat.at[part], new_sat_out.at[part], sems.at[1 + x // 4])
            copy.start()
            copies.append(copy)
    for copy in copies:
        copy.wait()


VMEM = pl.BlockSpec(memory_space=pltpu.VMEM)
HBM = pl.BlockSpec(memory_space=pltpu.HBM)


def call(kernel, outs, scratch, flops, args, far=0, out_spec=VMEM):
    args = [pltpu.with_memory_space_constraint(a, pltpu.HBM) for a in args[:far]] + args[far:]
    shapes = [jax.ShapeDtypeStruct(o[:-1], o[-1]) if isinstance(o[-1], type) else jax.ShapeDtypeStruct(o, jnp.float32) for o in outs]
    size = sum(a.size * a.dtype.itemsize for a in [*args, *shapes])
    return pl.pallas_call(
        kernel,
        out_shape=shapes,
        in_specs=[HBM] * far + [VMEM] * (len(args) - far),
        out_specs=[out_spec] * len(shapes),
        scratch_shapes=scratch,
        compiler_params=pltpu.CompilerParams(vmem_limit_bytes=24 * 1024 * 1024),
        cost_estimate=pl.CostEstimate(flops=flops, bytes_accessed=size, transcendentals=0),
    )(*args)


def space(*shape, dtype=jnp.float32):
    return pltpu.VMEM(shape, dtype)


def swaps(n, start):
    pairs = [(i, i + 1) for i in range(start, n - 1, 2)]
    return pairs + [(j, i) for i, j in pairs]


def on_device(pressure, saturation, source, permeability, pore_volume, basis, support, matrix):
    p_in, sat_in, src_in, pore_in = (
        a.reshape(-1, L) for a in (pressure, saturation, source, pore_volume)
    )
    perm_in = permeability.reshape(3, -1, L)
    basis_in = basis.reshape(-1, L)
    support = support.transpose(0, 2, 1).reshape(NX * K, NY)
    matrix = matrix.reshape(9 * NX, NY)
    n_narrow, n_wide = lax.axis_size("narrow"), lax.axis_size("wide")
    cells, fine, middle = NX * NY, NX * NY * K, (HIGH - LOW) * NY
    near = middle + 2 * NY
    out_even, out_odd, small, p, perm, bs, trans, basis = call(
        edge_kernel,
        [(N_ROWS, L), (N_ROWS, L), (SMALL * TALL, L), (cells, L), (3, cells, L), (K, cells, L), (3, cells, L),
         (fine, L, jnp.bfloat16)],
        [
            space(cells, L), space(fine, L), space(NX * K, NY, dtype=jnp.int32),
            space(9 * NX, NY), space(TALL, L), space(L, L), pltpu.SemaphoreType.DMA((12,)),
        ],
        10**7,
        [p_in, perm_in, src_in, basis_in, support, matrix, sat_in],
        far=7,
    )
    odd = lax.ppermute(out_odd, "narrow", swaps(n_narrow, 1))
    gathered = lax.all_gather(
        out_even, "narrow", axis_index_groups=[[i, i + 1] for i in range(0, n_narrow, 2)]
    )
    p_middle, perm_middle, bs_middle, trans_middle, acc, sat, frac, rate, basis_middle = call(
        middle_kernel,
        [
            (near, L), (3, near, L), (K, middle, L), (3, near, L), (TALL, L), (cells, L), (cells, L), (cells, L),
            (middle * K, L, jnp.bfloat16),
        ],
        [
            space(near, L), space(middle * K, L), space(cells, L),
            space(L, L), pltpu.SemaphoreType.DMA((6,)),
        ],
        10**7,
        [p_in, perm_in, src_in, basis_in, sat_in, pore_in, small],
        far=6,
    )
    sent_odd, sent_even, small = call(
        narrow_kernel,
        [(W_ROWS, L), (W_ROWS, L), (SMALL * TALL, L)],
        [space(L, L)],
        10**6,
        [gathered, odd, p, perm, bs, p_middle, perm_middle, bs_middle, sat, small, acc],
    )
    in_odd = lax.ppermute(sent_odd, "wide", swaps(n_wide, 1))
    in_even = lax.ppermute(sent_even, "wide", swaps(n_wide, 0))
    new, new_sat = call(
        final_kernel,
        [(cells, L), (cells, L)],
        [space(cells, L), space(cells, L), space(L, L), pltpu.SemaphoreType.DMA((5,))],
        10**7,
        [
            in_odd, in_even, sent_odd, sent_even, gathered, odd, small, p, perm, basis, trans,
            p_middle, basis_middle, trans_middle, sat, frac, rate,
        ],
        out_spec=HBM,
    )
    return new.reshape(pressure.shape), new_sat.reshape(pressure.shape)


def solution(mesh):
    return jax.shard_map(
        on_device,
        mesh=mesh,
        in_specs=(
            P("narrow", "wide", None),
            P("narrow", "wide", None),
            P("narrow", "wide", None),
            P(None, "narrow", "wide", None),
            P("narrow", "wide", None),
            P("narrow", "wide", None, None),
            P("narrow", "wide", None),
            P(None, "narrow", "wide"),
        ),
        out_specs=(P("narrow", "wide", None), P("narrow", "wide", None)),
        check_vma=False,
    )
```

```python
import jax
import jax.numpy as jnp
from jax import lax
from jax.experimental import pallas as pl
from jax.experimental.pallas import tpu as pltpu
from jax.sharding import PartitionSpec as P

SWEEPS = 3
OFFSETS = [(o // 3 - 1, o % 3 - 1) for o in range(9)]
OMEGA = 0.6667
DT = 0.01

NX, NY, L, K = 16, 32, 128, 4
TOP, WEST, TALL = 8, 4, 32
EDGE = 5
FIELDS = 2 + K
SUP, MAT, ACC = 0, K, K + 9
SMALL = K + 10
N_P, N_K, N_S, N_B, N_C = 0, 32, 64, 96, 224
N_SMALL = 288
N_ROWS = N_SMALL + 8 * 5
COLUMN = NX + 2 * EDGE
MARGIN = TOP - EDGE
W_SAT = 0
W_FIELD = NX
W_SMALL = W_FIELD + FIELDS * COLUMN
W_ROWS = W_SMALL + COLUMN + 10


def roll(a, shift, axis):
    shift %= a.shape[axis]
    return pltpu.roll(a, shift, axis) if shift else a


def iota(shape, axis):
    return lax.broadcasted_iota(jnp.int32, shape, axis)


def trans_of(here, there):
    return 2.0 * here * there / (here + there)


def fraction(sat):
    rest = 1.0 - sat
    square = sat * sat
    return square / (square + 0.5 * (rest * rest))


def lane_sum(a):
    return jnp.sum(a, axis=-1, keepdims=True)


def halves(a):
    high = a.astype(jnp.bfloat16)
    return high, (a - high.astype(jnp.float32)).astype(jnp.bfloat16)


def bin_pieces(sup, pieces):
    total = None
    for dy in (-1, 0, 1):
        column = None
        for dx in (-1, 0, 1):
            code = float((dx + 1) * 3 + dy + 1)
            part = None
            for k in range(K):
                term = jnp.where(sup[k] == code, pieces[k], 0.0)
                part = term if part is None else part + term
            part = roll(part, dx, 0)
            column = part if column is None else column + part
        column = roll(column, dy, 1)
        total = column if total is None else total + column
    return total


def turned(scratch, value):
    scratch[...] = jnp.zeros((L, L), jnp.float32)
    scratch[WEST : WEST + NY, :] = value
    return scratch[...].T


def rows_residual(p, perm, src, trans, lo, hi, base):
    rows, lanes = iota((NY, L), 0), iota((NY, L), 1)

    def face(x):
        a, b = slice((x - base) * NY, (x - base + 1) * NY), slice((x - base + 1) * NY, (x - base + 2) * NY)
        value = trans_of(perm[0, a, :], perm[0, b, :])
        trans[0, a, :] = value
        return value * (p[a, :] - p[b, :])

    result = []
    last = face(lo - 1) if lo > 0 else None
    for x in range(lo, hi):
        at = slice((x - base) * NY, (x - base + 1) * NY)
        here, ky, kz = p[at, :], perm[1, at, :], perm[2, at, :]
        ty = jnp.where(rows < NY - 1, trans_of(ky, roll(ky, -1, 0)), 0.0)
        tz = jnp.where(lanes < L - 1, trans_of(kz, roll(kz, -1, 1)), 0.0)
        trans[1, at, :] = ty
        trans[2, at, :] = tz
        fy = ty * (here - roll(here, -1, 0))
        fz = tz * (here - roll(here, -1, 1))
        total = (fy - roll(fy, 1, 0)) + (fz - roll(fz, 1, 1))
        if last is not None:
            total = total - last
        last = None
        if x < NX - 1:
            last = face(x)
            total = total + last
        result.append(src[at, :] - total)
    return result


def add_pieces(pieces, residuals, lo, mixed, bs, base):
    lanes = iota((NY, L), 1)
    for i, res in enumerate(residuals):
        x = lo + i
        for k in range(K):
            b = mixed[pl.ds((x - base) * NY * K + k, NY, stride=K), :]
            bs[k, (x - base) * NY : (x - base + 1) * NY, :] = b
            pieces = jnp.where(lanes == k * TALL + TOP + x, lane_sum(b * res), pieces)
    return pieces


def split_pieces(square, pieces):
    flipped = turned(square, pieces)
    return [flipped[k * TALL : (k + 1) * TALL, :] for k in range(K)]


LOW, HIGH = EDGE, NX - EDGE


def copies_of(sems, pairs):
    out = [pltpu.make_async_copy(src, dst, sems.at[i]) for i, (src, dst) in enumerate(pairs)]
    for copy in out:
        copy.start()
    return out


def edge_kernel(
    p_in, perm_in, src_in, basis_in, support_in, matrix_in, sat_in,
    out_even, out_odd, small, p, perm, bs, trans, basis,
    src, mixed, support, matrix, place, square, sems,
):
    even = lax.axis_index("narrow") % 2 == 0
    rows_even = pl.ds(pl.multiple_of(jnp.where(even, NX - 1, 0) * NY, NY), NY)
    rows_odd = pl.ds(pl.multiple_of(jnp.where(even, 0, NX - 1) * NY, NY), NY)
    pairs = []
    for near, first in ((0, 0), (HIGH - 1, HIGH)):
        part = pl.ds(near * NY, (EDGE + 1) * NY)
        own, fine = pl.ds(first * NY, EDGE * NY), pl.ds(first * NY * K, EDGE * NY * K)
        pairs += [(p_in.at[part], p.at[part]), (perm_in.at[:, part], perm.at[:, part])]
        pairs += [(src_in.at[own], src.at[own]), (basis_in.at[fine], basis.at[fine])]
    pairs += [(support_in, support), (matrix_in, matrix)]
    pairs += [(sat_in.at[rows_even], out_even.at[pl.ds(N_S, NY)])]
    pairs += [(sat_in.at[rows_odd], out_odd.at[pl.ds(N_S, NY)])]
    copies = copies_of(sems, pairs)
    pieces = jnp.zeros((NY, L), jnp.float32)
    for i, first in enumerate((0, HIGH)):
        for copy in copies[4 * i : 4 * i + 3]:
            copy.wait()
        residuals = rows_residual(p, perm, src, trans, first, first + EDGE, 0)
        copies[4 * i + 3].wait()
        fine = slice(first * NY * K, (first + EDGE) * NY * K)
        mixed[fine, :] = basis[fine, :].astype(jnp.float32)
        pieces = add_pieces(pieces, residuals, first, mixed, bs, 0)
    pieces = split_pieces(square, pieces)
    copies[8].wait()
    copies[9].wait()
    place[...] = jnp.zeros((TALL, L), jnp.float32)
    stack = []
    for i in range(K + 9):
        if i < MAT:
            value = support[pl.ds(i, NX, stride=K), :].astype(jnp.float32)
        else:
            value = matrix[(i - MAT) * NX : (i - MAT + 1) * NX, :]
        place[TOP : TOP + NX, 0:NY] = value
        stack.append(roll(place[...], WEST, 1))
    acc = bin_pieces(stack[:K], pieces)
    stack.append(acc)
    for i in range(SMALL):
        small[i * TALL : (i + 1) * TALL, :] = stack[i]
    for out, takes_last in ((out_even, even), (out_odd, jnp.logical_not(even))):
        edge = jnp.where(takes_last, NX - 1, 0)
        row = pl.multiple_of(edge * NY, NY)
        out[N_P : N_P + NY, :] = p[pl.ds(row, NY), :]
        out[N_K : N_K + NY, :] = perm[0, pl.ds(row, NY), :]
        for k in range(K):
            out[N_B + k * NY : N_B + (k + 1) * NY, :] = bs[k, pl.ds(row, NY), :]
        start = jnp.where(takes_last, NX - EDGE, 0) * NY
        for c, col in enumerate((0, NY - 1)):
            fields = [
                p[pl.ds(start + col, EDGE, stride=NY), :],
                perm[1, pl.ds(start + col, EDGE, stride=NY), :],
            ] + [bs[k, pl.ds(start + col, EDGE, stride=NY), :] for k in range(K)]
            for f, value in enumerate(fields):
                to = N_C + (f * 2 + c) * EDGE
                out[to : to + EDGE, :] = value
        window = [jnp.where(takes_last, s[16:24, :], s[8:16, :]) for s in stack]
        window.append(jnp.where(takes_last, acc[24:32, :], acc[0:8, :]))
        for i in range(5):
            a, b, c = window[3 * i : 3 * i + 3]
            out[N_SMALL + 8 * i : N_SMALL + 8 * i + 8, :] = a + roll(b, 40, 1) + roll(c, 80, 1)
    copies[10].wait()
    copies[11].wait()


def middle_kernel(
    p_in, perm_in, src_in, basis_in, sat_in, pore_in, small,
    p, perm, bs, trans, acc, sat, frac, rate, basis,
    src, mixed, pore, square, sems,
):
    near = pl.ds((LOW - 1) * NY, (HIGH - LOW + 2) * NY)
    own, fine = pl.ds(LOW * NY, (HIGH - LOW) * NY), pl.ds(LOW * NY * K, (HIGH - LOW) * NY * K)
    inner = pl.ds(NY, (HIGH - LOW) * NY)
    copies = copies_of(
        sems,
        [
            (p_in.at[near], p), (perm_in.at[:, near], perm), (src_in.at[own], src.at[inner]),
            (basis_in.at[fine], basis), (sat_in, sat), (pore_in, pore),
        ],
    )
    for copy in copies[:3]:
        copy.wait()
    residuals = rows_residual(p, perm, src, trans, LOW, HIGH, LOW - 1)
    copies[3].wait()
    mixed[...] = basis[...].astype(jnp.float32)
    pieces = add_pieces(jnp.zeros((NY, L), jnp.float32), residuals, LOW, mixed, bs, LOW)
    sup = [small[k * TALL : (k + 1) * TALL, :] for k in range(K)]
    acc[...] = bin_pieces(sup, split_pieces(square, pieces))
    copies[4].wait()
    frac[...] = fraction(sat[...])
    copies[5].wait()
    rate[...] = DT / pore[...]


def narrow_kernel(
    gathered, odd, p, perm, bs, p_middle, perm_middle, bs_middle, sat, small, acc_middle, out_odd, out_even, small_out, square
):
    even = lax.axis_index("narrow") % 2 == 0
    wide_even = lax.axis_index("wide") % 2 == 0
    mate = jnp.where(even, 1, 0)
    lanes = iota((NY, L), 1)

    def before(lo, n):
        return jnp.where(even, odd[lo : lo + n, :], gathered[mate, lo : lo + n, :])

    def after(lo, n):
        return jnp.where(even, gathered[mate, lo : lo + n, :], odd[lo : lo + n, :])

    in_slot = iota((8, L), 1) < 40

    def windows(get):
        out = []
        for i in range(5):
            block = get(N_SMALL + 8 * i, 8)
            out += [jnp.where(in_slot, roll(block, -40 * j, 1), 0.0) for j in range(3)]
        return out

    top, bottom = windows(before), windows(after)
    none = jnp.zeros((8, L), jnp.float32)
    stack = []
    for i in range(SMALL):
        own = small[i * TALL : (i + 1) * TALL, :]
        if i < ACC:
            own = own[8:24, :]
            stack.append(jnp.concatenate([top[i], own, bottom[i]], axis=0))
        else:
            stack.append(own + jnp.concatenate([top[i], top[i + 1], bottom[i + 1], bottom[i]], axis=0))
    pieces = jnp.zeros((NY, L), jnp.float32)
    for x, other_x, get in ((0, -1, before), (NX - 1, NX, after)):
        at = x * NY
        flux = trans_of(perm[0, at : at + NY, :], get(N_K, NY)) * (p[at : at + NY, :] - get(N_P, NY))
        for k in range(K):
            mine = lane_sum(bs[k, at : at + NY, :] * -flux)
            pieces = jnp.where(lanes == k * TALL + TOP + x, mine, pieces)
            other = lane_sum(get(N_B + k * NY, NY) * flux)
            pieces = jnp.where(lanes == k * TALL + TOP + other_x, other, pieces)
    stack[ACC] = stack[ACC] + acc_middle[...] + bin_pieces(stack[:K], split_pieces(square, pieces))
    for i in range(SMALL):
        small_out[i * TALL : (i + 1) * TALL, :] = stack[i]
    slot = iota((TALL, L), 1) // 8
    first = jnp.zeros((TALL, L), jnp.float32)
    last = jnp.zeros((TALL, L), jnp.float32)
    for i in range(SMALL):
        first = jnp.where(slot == i, roll(stack[i], 8 * i, 1), first)
        last = jnp.where(slot == i, roll(stack[i], 8 * i - 32, 1), last)
    for out, takes_last in ((out_even, wide_even), (out_odd, jnp.logical_not(wide_even))):
        col = jnp.where(takes_last, NY - 1, 0)
        for f in range(FIELDS):
            base = W_FIELD + f * COLUMN
            lo = N_C + f * 2 * EDGE
            out[base : base + EDGE, :] = jnp.where(takes_last, before(lo + EDGE, EDGE), before(lo, EDGE))
            base += EDGE
            for middle, x, n in ((False, 0, LOW), (True, LOW, HIGH - LOW), (False, HIGH, NX - HIGH)):
                rows = pl.ds((x - LOW) * NY + col if middle else x * NY + col, n, stride=NY)
                after_first = pl.ds((x - LOW + 1) * NY + col if middle else x * NY + col, n, stride=NY)
                if f == 0:
                    column = (p_middle if middle else p)[after_first, :]
                elif f == 1:
                    column = (perm_middle if middle else perm)[1, after_first, :]
                else:
                    column = (bs_middle if middle else bs)[f - 2, rows, :]
                out[base + x : base + x + n, :] = column
            base += NX
            out[base : base + EDGE, :] = jnp.where(takes_last, after(lo + EDGE, EDGE), after(lo, EDGE))
        out[W_SAT : W_SAT + NX, :] = sat[pl.ds(col, NX, stride=NY), :]
        out[W_SMALL : W_SMALL + COLUMN, :] = jnp.where(takes_last, last, first)[MARGIN : MARGIN + COLUMN, :]
        out[W_SMALL + COLUMN : W_ROWS, :] = jnp.zeros((W_ROWS - W_SMALL - COLUMN, L), jnp.float32)


def final_kernel(
    in_odd, in_even, sent_odd, sent_even, gathered, odd, small, p, perm, basis, trans,
    p_middle, basis_middle, trans_middle, sat, frac, rate,
    new_out, new_sat_out,
    new, new_sat, square, sems,
):
    even = lax.axis_index("narrow") % 2 == 0
    wide_even = lax.axis_index("wide") % 2 == 0
    mate = jnp.where(even, 1, 0)

    def before(lo, n):
        return jnp.where(even, odd[lo : lo + n, :], gathered[mate, lo : lo + n, :])

    def after(lo, n):
        return jnp.where(even, gathered[mate, lo : lo + n, :], odd[lo : lo + n, :])

    wide_mate = jnp.where(wide_even, 1, 0)

    def left(lo, n):
        return jnp.where(wide_even, in_odd[lo : lo + n, :], in_even[wide_mate, lo : lo + n, :])

    def right(lo, n):
        return jnp.where(wide_even, in_even[wide_mate, lo : lo + n, :], in_odd[lo : lo + n, :])

    def first(lo, n):
        return jnp.where(wide_even, sent_odd[lo : lo + n, :], sent_even[lo : lo + n, :])

    def last(lo, n):
        return jnp.where(wide_even, sent_even[lo : lo + n, :], sent_odd[lo : lo + n, :])

    lane = iota((TALL, L), 1)
    row = iota((TALL, L), 0)
    sent = jnp.logical_and(row >= MARGIN, row < MARGIN + COLUMN)

    def column_of(get, f):
        return get(W_FIELD + f * COLUMN - MARGIN, TALL)

    def own_rows(get, f):
        return get(W_FIELD + f * COLUMN + EDGE, NX)

    from_left, from_right = (jnp.where(sent, column_of(get, FIELDS), 0.0) for get in (left, right))
    stack = []
    for i in range(SMALL):
        own = small[i * TALL : (i + 1) * TALL, :]
        own = own + jnp.where(lane < 8, roll(from_left, -8 * i, 1), 0.0)
        own = own + jnp.where(lane // 8 == 4, roll(from_right, 32 - 8 * i, 1), 0.0)
        stack.append(own)
    sup, mat = stack[:K], stack[MAT : MAT + 9]
    pieces = [jnp.zeros((TALL, L), jnp.float32)] * K
    for mine, other, y, other_y in ((first, left, 0, -1), (last, right, NY - 1, NY)):
        k_here, k_there = column_of(mine, 1), column_of(other, 1)
        total = k_here + k_there
        flux = (2.0 * k_here * k_there / jnp.where(total > 0, total, 1.0)) * (
            column_of(mine, 0) - column_of(other, 0)
        )
        for k in range(K):
            here = lane_sum(column_of(mine, 2 + k) * -flux)
            there = lane_sum(column_of(other, 2 + k) * flux)
            pieces[k] = jnp.where(lane == WEST + y, here, pieces[k])
            pieces[k] = jnp.where(lane == WEST + other_y, there, pieces[k])
    res = stack[ACC] + bin_pieces(sup, pieces)
    diag = mat[4]
    scale = jnp.where(diag > 0, OMEGA / jnp.where(diag > 0, diag, 1.0), 0.0)

    def moved(coarse):
        sides = {dy: roll(coarse, -dy, 1) for dy in (-1, 0, 1)}
        return [roll(sides[dy], -dx, 0) for dx, dy in OFFSETS]

    coarse = scale * res
    for _ in range(SWEEPS - 1):
        rest = res
        for o, value in enumerate(moved(coarse)):
            rest = rest - mat[o] * value
        coarse = coarse + scale * rest
    shifts = moved(coarse)
    picked = []
    for k in range(K):
        total = jnp.zeros((TALL, L), jnp.float32)
        for o in range(9):
            total = jnp.where(sup[k] == float(o), shifts[o], total)
        picked.append(total)
    spread = jnp.zeros((TALL, L), jnp.float32)
    for k in range(K):
        spread = jnp.where(lane // NY == k, roll(picked[k], k * NY - WEST, 1), spread)
    spread = jnp.concatenate(halves(spread), axis=0)
    source = iota((L, L), 0)
    reorder = iota((L, L), 1) == (source % NY) * K + source // NY
    square[0 : 2 * TALL, :] = jnp.dot(
        spread, reorder.astype(jnp.bfloat16), preferred_element_type=jnp.float32
    )
    square[2 * TALL :, :] = spread.astype(jnp.float32)
    rows, lanes = iota((NY, L), 0), iota((NY, L), 1)

    def prolonged(values, start, x, mine):
        parts = []
        for at in (start, start + TALL):
            parts.append(jnp.where(mine, square[at + TOP + x : at + TOP + x + 1, :], 0.0))
        weights = jnp.concatenate(parts, axis=0).astype(jnp.bfloat16)
        both = jnp.dot(weights, values, preferred_element_type=jnp.float32)
        return both[:NY, :] + both[NY:, :]

    own = lanes // K == rows
    for x in range(NX):
        at = slice(x * NY, (x + 1) * NY)
        inner = LOW <= x < HIGH
        before_x = p_middle[(x - LOW + 1) * NY : (x - LOW + 2) * NY, :] if inner else p[at, :]
        ref, base = (basis_middle, LOW) if inner else (basis, 0)
        values = ref[(x - base) * NY * K : (x - base + 1) * NY * K, :]
        new[at, :] = before_x + prolonged(values, 0, x, own)
    copies = copies_of(sems, [(new, new_out)])
    ends = []
    own = lanes % NY == rows
    for get, x in ((before, -1), (after, NX)):
        values = get(N_B, K * NY).astype(jnp.bfloat16)
        ends.append(get(N_P, NY) + prolonged(values, 2 * TALL, x, own))
    sides = []
    for get, y in ((left, -1), (right, NY)):
        total = own_rows(get, 0)
        for k in range(K):
            column = picked[k][TOP : TOP + NX, WEST + y : WEST + y + 1]
            total = total + own_rows(get, 2 + k) * column
        sides.append(total)

    def carried(value, here, there, f_here, f_there):
        flux = value * (here - there)
        return flux * jnp.where(flux > 0, f_here, f_there)

    west_f, east_f = fraction(left(W_SAT, NX)), fraction(right(W_SAT, NX))
    east_t = trans_of(own_rows(last, 1), own_rows(right, 1))
    west_flow = carried(
        trans_of(own_rows(first, 1), own_rows(left, 1)),
        sides[0],
        new[pl.ds(0, NX, stride=NY), :],
        west_f,
        frac[pl.ds(0, NX, stride=NY), :],
    )
    end = rows == NY - 1
    p_here, f_here = new[0:NY, :], frac[0:NY, :]
    flow_in = carried(
        trans_of(before(N_K, NY), perm[0, 0:NY, :]), ends[0], p_here, fraction(before(N_S, NY)), f_here
    )
    for x in range(NX):
        at = slice(x * NY, (x + 1) * NY)
        ref, base = (trans_middle, LOW - 1) if LOW <= x < HIGH else (trans, 0)
        tx, ty, tz = (ref[c, (x - base) * NY : (x - base + 1) * NY, :] for c in range(3))
        if x < NX - 1:
            nxt = slice((x + 1) * NY, (x + 2) * NY)
            p_next, f_next = new[nxt, :], frac[nxt, :]
        else:
            p_next, f_next = ends[1], fraction(after(N_S, NY))
            tx = trans_of(perm[0, at, :], after(N_K, NY))
        flow_out = carried(tx, p_here, p_next, f_here, f_next)
        total = flow_out - flow_in
        flow_in = flow_out
        beside = lambda a, e: jnp.where(end, e[x : x + 1, :], roll(a, -1, 0))
        fy = carried(
            jnp.where(end, east_t[x : x + 1, :], ty),
            p_here,
            beside(p_here, sides[1]),
            f_here,
            beside(f_here, east_f),
        )
        total = total + (fy - jnp.where(rows == 0, west_flow[x : x + 1, :], roll(fy, 1, 0)))
        fz = carried(tz, p_here, roll(p_here, -1, 1), f_here, roll(f_here, -1, 1))
        total = total + (fz - roll(fz, 1, 1))
        new_sat[at, :] = sat[at, :] - rate[at, :] * total
        p_here, f_here = p_next, f_next
        if x % 4 == 3:
            part = pl.ds((x - 3) * NY, 4 * NY)
            copy = pltpu.make_async_copy(new_sat.at[part], new_sat_out.at[part], sems.at[1 + x // 4])
            copy.start()
            copies.append(copy)
    for copy in copies:
        copy.wait()


VMEM = pl.BlockSpec(memory_space=pltpu.VMEM)
HBM = pl.BlockSpec(memory_space=pltpu.HBM)


def call(kernel, outs, scratch, flops, args, far=0, out_spec=VMEM):
    args = [pltpu.with_memory_space_constraint(a, pltpu.HBM) for a in args[:far]] + args[far:]
    shapes = [jax.ShapeDtypeStruct(o[:-1], o[-1]) if isinstance(o[-1], type) else jax.ShapeDtypeStruct(o, jnp.float32) for o in outs]
    size = sum(a.size * a.dtype.itemsize for a in [*args, *shapes])
    return pl.pallas_call(
        kernel,
        out_shape=shapes,
        in_specs=[HBM] * far + [VMEM] * (len(args) - far),
        out_specs=[out_spec] * len(shapes),
        scratch_shapes=scratch,
        compiler_params=pltpu.CompilerParams(vmem_limit_bytes=24 * 1024 * 1024),
        cost_estimate=pl.CostEstimate(flops=flops, bytes_accessed=size, transcendentals=0),
    )(*args)


def space(*shape, dtype=jnp.float32):
    return pltpu.VMEM(shape, dtype)


def swaps(n, start):
    pairs = [(i, i + 1) for i in range(start, n - 1, 2)]
    return pairs + [(j, i) for i, j in pairs]


def on_device(pressure, saturation, source, permeability, pore_volume, basis, support, matrix):
    p_in, sat_in, src_in, pore_in = (
        a.reshape(-1, L) for a in (pressure, saturation, source, pore_volume)
    )
    perm_in = permeability.reshape(3, -1, L)
    basis_in = basis.reshape(-1, L)
    support = support.transpose(0, 2, 1).reshape(NX * K, NY)
    matrix = matrix.reshape(9 * NX, NY)
    n_narrow, n_wide = lax.axis_size("narrow"), lax.axis_size("wide")
    cells, fine, middle = NX * NY, NX * NY * K, (HIGH - LOW) * NY
    near = middle + 2 * NY
    out_even, out_odd, small, p, perm, bs, trans, basis = call(
        edge_kernel,
        [(N_ROWS, L), (N_ROWS, L), (SMALL * TALL, L), (cells, L), (3, cells, L), (K, cells, L), (3, cells, L),
         (fine, L, jnp.bfloat16)],
        [
            space(cells, L), space(fine, L), space(NX * K, NY, dtype=jnp.int32),
            space(9 * NX, NY), space(TALL, L), space(L, L), pltpu.SemaphoreType.DMA((12,)),
        ],
        10**7,
        [p_in, perm_in, src_in, basis_in, support, matrix, sat_in],
        far=7,
    )
    odd = lax.ppermute(out_odd, "narrow", swaps(n_narrow, 1))
    gathered = lax.all_gather(
        out_even, "narrow", axis_index_groups=[[i, i + 1] for i in range(0, n_narrow, 2)]
    )
    p_middle, perm_middle, bs_middle, trans_middle, acc, sat, frac, rate, basis_middle = call(
        middle_kernel,
        [
            (near, L), (3, near, L), (K, middle, L), (3, near, L), (TALL, L), (cells, L), (cells, L), (cells, L),
            (middle * K, L, jnp.bfloat16),
        ],
        [
            space(near, L), space(middle * K, L), space(cells, L),
            space(L, L), pltpu.SemaphoreType.DMA((6,)),
        ],
        10**7,
        [p_in, perm_in, src_in, basis_in, sat_in, pore_in, small],
        far=6,
    )
    sent_odd, sent_even, small = call(
        narrow_kernel,
        [(W_ROWS, L), (W_ROWS, L), (SMALL * TALL, L)],
        [space(L, L)],
        10**6,
        [gathered, odd, p, perm, bs, p_middle, perm_middle, bs_middle, sat, small, acc],
    )
    in_odd = lax.ppermute(sent_odd, "wide", swaps(n_wide, 1))
    in_even = lax.all_gather(
        sent_even, "wide", axis_index_groups=[[i, i + 1] for i in range(0, n_wide, 2)]
    )
    new, new_sat = call(
        final_kernel,
        [(cells, L), (cells, L)],
        [space(cells, L), space(cells, L), space(L, L), pltpu.SemaphoreType.DMA((5,))],
        10**7,
        [
            in_odd, in_even, sent_odd, sent_even, gathered, odd, small, p, perm, basis, trans,
            p_middle, basis_middle, trans_middle, sat, frac, rate,
        ],
        out_spec=HBM,
    )
    return new.reshape(pressure.shape), new_sat.reshape(pressure.shape)


def solution(mesh):
    return jax.shard_map(
        on_device,
        mesh=mesh,
        in_specs=(
            P("narrow", "wide", None),
            P("narrow", "wide", None),
            P("narrow", "wide", None),
            P(None, "narrow", "wide", None),
            P("narrow", "wide", None),
            P("narrow", "wide", None, None),
            P("narrow", "wide", None),
            P(None, "narrow", "wide"),
        ),
        out_specs=(P("narrow", "wide", None), P("narrow", "wide", None)),
        check_vma=False,
    )
```

```python
import jax
import jax.numpy as jnp
from jax import lax
from jax.experimental import pallas as pl
from jax.experimental.pallas import tpu as pltpu
from jax.sharding import PartitionSpec as P

SWEEPS = 3
OFFSETS = [(o // 3 - 1, o % 3 - 1) for o in range(9)]
OMEGA = 0.6667
DT = 0.01

NX, NY, L, K = 16, 32, 128, 4
TOP, WEST, TALL = 8, 4, 32
EDGE = 5
FIELDS = 2 + K
SUP, MAT, ACC = 0, K, K + 9
SMALL = K + 10
N_P, N_K, N_S, N_B, N_C = 0, 32, 64, 96, 224
N_SMALL = 288
N_ROWS = N_SMALL + 8 * 5
COLUMN = NX + 2 * EDGE
MARGIN = TOP - EDGE
W_SAT = 0
W_FIELD = NX
W_SMALL = W_FIELD + FIELDS * COLUMN
W_ROWS = W_SMALL + COLUMN + 10


def roll(a, shift, axis):
    shift %= a.shape[axis]
    return pltpu.roll(a, shift, axis) if shift else a


def iota(shape, axis):
    return lax.broadcasted_iota(jnp.int32, shape, axis)


def trans_of(here, there):
    return 2.0 * here * there / (here + there)


def fraction(sat):
    rest = 1.0 - sat
    square = sat * sat
    return square / (square + 0.5 * (rest * rest))


def lane_sum(a):
    return jnp.sum(a, axis=-1, keepdims=True)


def halves(a):
    high = a.astype(jnp.bfloat16)
    return high, (a - high.astype(jnp.float32)).astype(jnp.bfloat16)


def bin_pieces(sup, pieces):
    total = None
    for dy in (-1, 0, 1):
        column = None
        for dx in (-1, 0, 1):
            code = float((dx + 1) * 3 + dy + 1)
            part = None
            for k in range(K):
                term = jnp.where(sup[k] == code, pieces[k], 0.0)
                part = term if part is None else part + term
            part = roll(part, dx, 0)
            column = part if column is None else column + part
        column = roll(column, dy, 1)
        total = column if total is None else total + column
    return total


def turned(scratch, value):
    scratch[...] = jnp.zeros((L, L), jnp.float32)
    scratch[WEST : WEST + NY, :] = value
    return scratch[...].T


def rows_residual(p, perm, src, trans, lo, hi, base):
    rows, lanes = iota((NY, L), 0), iota((NY, L), 1)

    def face(x):
        a, b = slice((x - base) * NY, (x - base + 1) * NY), slice((x - base + 1) * NY, (x - base + 2) * NY)
        value = trans_of(perm[0, a, :], perm[0, b, :])
        trans[0, a, :] = value
        return value * (p[a, :] - p[b, :])

    result = []
    last = face(lo - 1) if lo > 0 else None
    for x in range(lo, hi):
        at = slice((x - base) * NY, (x - base + 1) * NY)
        here, ky, kz = p[at, :], perm[1, at, :], perm[2, at, :]
        ty = jnp.where(rows < NY - 1, trans_of(ky, roll(ky, -1, 0)), 0.0)
        tz = jnp.where(lanes < L - 1, trans_of(kz, roll(kz, -1, 1)), 0.0)
        trans[1, at, :] = ty
        trans[2, at, :] = tz
        fy = ty * (here - roll(here, -1, 0))
        fz = tz * (here - roll(here, -1, 1))
        total = (fy - roll(fy, 1, 0)) + (fz - roll(fz, 1, 1))
        if last is not None:
            total = total - last
        last = None
        if x < NX - 1:
            last = face(x)
            total = total + last
        result.append(src[at, :] - total)
    return result


def add_pieces(pieces, residuals, lo, mixed, bs, base):
    lanes = iota((NY, L), 1)
    for i, res in enumerate(residuals):
        x = lo + i
        for k in range(K):
            b = mixed[pl.ds((x - base) * NY * K + k, NY, stride=K), :]
            bs[k, (x - base) * NY : (x - base + 1) * NY, :] = b
            pieces = jnp.where(lanes == k * TALL + TOP + x, lane_sum(b * res), pieces)
    return pieces


def split_pieces(square, pieces):
    flipped = turned(square, pieces)
    return [flipped[k * TALL : (k + 1) * TALL, :] for k in range(K)]


CHUNKS = (4, 9, 13, NX - 1)
LOW, HIGH = EDGE, NX - EDGE


def copies_of(sems, pairs):
    out = [pltpu.make_async_copy(src, dst, sems.at[i]) for i, (src, dst) in enumerate(pairs)]
    for copy in out:
        copy.start()
    return out


def edge_kernel(
    p_in, perm_in, src_in, basis_in, support_in, matrix_in, sat_in,
    out_even, out_odd, small, p, perm, bs, trans, basis,
    src, mixed, support, matrix, place, square, sems,
):
    even = lax.axis_index("narrow") % 2 == 0
    rows_even = pl.ds(pl.multiple_of(jnp.where(even, NX - 1, 0) * NY, NY), NY)
    rows_odd = pl.ds(pl.multiple_of(jnp.where(even, 0, NX - 1) * NY, NY), NY)
    pairs = [(support_in, support), (matrix_in, matrix)]
    for near, first in ((0, 0), (HIGH - 1, HIGH)):
        part = pl.ds(near * NY, (EDGE + 1) * NY)
        own, fine = pl.ds(first * NY, EDGE * NY), pl.ds(first * NY * K, EDGE * NY * K)
        pairs += [(p_in.at[part], p.at[part]), (perm_in.at[:, part], perm.at[:, part])]
        pairs += [(src_in.at[own], src.at[own]), (basis_in.at[fine], basis.at[fine])]
    pairs += [(sat_in.at[rows_even], out_even.at[pl.ds(N_S, NY)])]
    pairs += [(sat_in.at[rows_odd], out_odd.at[pl.ds(N_S, NY)])]
    copies = copies_of(sems, pairs)
    copies[0].wait()
    copies[1].wait()
    place[...] = jnp.zeros((TALL, L), jnp.float32)
    for i in range(K + 9):
        if i < MAT:
            value = support[pl.ds(i, NX, stride=K), :].astype(jnp.float32)
        else:
            value = matrix[(i - MAT) * NX : (i - MAT + 1) * NX, :]
        place[TOP : TOP + NX, 0:NY] = value
        small[i * TALL : (i + 1) * TALL, :] = roll(place[...], WEST, 1)
    pieces = jnp.zeros((NY, L), jnp.float32)
    for i, first in enumerate((0, HIGH)):
        for copy in copies[4 * i + 2 : 4 * i + 5]:
            copy.wait()
        residuals = rows_residual(p, perm, src, trans, first, first + EDGE, 0)
        copies[4 * i + 5].wait()
        fine = slice(first * NY * K, (first + EDGE) * NY * K)
        mixed[fine, :] = basis[fine, :].astype(jnp.float32)
        pieces = add_pieces(pieces, residuals, first, mixed, bs, 0)
    pieces = split_pieces(square, pieces)
    stack = [small[i * TALL : (i + 1) * TALL, :] for i in range(ACC)]
    acc = bin_pieces(stack[:K], pieces)
    stack.append(acc)
    small[ACC * TALL : SMALL * TALL, :] = acc
    for out, takes_last in ((out_even, even), (out_odd, jnp.logical_not(even))):
        edge = jnp.where(takes_last, NX - 1, 0)
        row = pl.multiple_of(edge * NY, NY)
        out[N_P : N_P + NY, :] = p[pl.ds(row, NY), :]
        out[N_K : N_K + NY, :] = perm[0, pl.ds(row, NY), :]
        for k in range(K):
            out[N_B + k * NY : N_B + (k + 1) * NY, :] = bs[k, pl.ds(row, NY), :]
        start = jnp.where(takes_last, NX - EDGE, 0) * NY
        for c, col in enumerate((0, NY - 1)):
            fields = [
                p[pl.ds(start + col, EDGE, stride=NY), :],
                perm[1, pl.ds(start + col, EDGE, stride=NY), :],
            ] + [bs[k, pl.ds(start + col, EDGE, stride=NY), :] for k in range(K)]
            for f, value in enumerate(fields):
                to = N_C + (f * 2 + c) * EDGE
                out[to : to + EDGE, :] = value
        window = [jnp.where(takes_last, s[16:24, :], s[8:16, :]) for s in stack]
        window.append(jnp.where(takes_last, acc[24:32, :], acc[0:8, :]))
        for i in range(5):
            a, b, c = window[3 * i : 3 * i + 3]
            out[N_SMALL + 8 * i : N_SMALL + 8 * i + 8, :] = a + roll(b, 40, 1) + roll(c, 80, 1)
    copies[10].wait()
    copies[11].wait()


def middle_kernel(
    p_in, perm_in, src_in, basis_in, sat_in, pore_in, small,
    p, perm, bs, trans, acc, sat, frac, rate, basis,
    src, mixed, pore, square, sems,
):
    near = pl.ds((LOW - 1) * NY, (HIGH - LOW + 2) * NY)
    own, fine = pl.ds(LOW * NY, (HIGH - LOW) * NY), pl.ds(LOW * NY * K, (HIGH - LOW) * NY * K)
    inner = pl.ds(NY, (HIGH - LOW) * NY)
    copies = copies_of(
        sems,
        [
            (p_in.at[near], p), (perm_in.at[:, near], perm), (src_in.at[own], src.at[inner]),
            (basis_in.at[fine], basis), (sat_in, sat), (pore_in, pore),
        ],
    )
    for copy in copies[:3]:
        copy.wait()
    residuals = rows_residual(p, perm, src, trans, LOW, HIGH, LOW - 1)
    copies[3].wait()
    mixed[...] = basis[...].astype(jnp.float32)
    pieces = add_pieces(jnp.zeros((NY, L), jnp.float32), residuals, LOW, mixed, bs, LOW)
    sup = [small[k * TALL : (k + 1) * TALL, :] for k in range(K)]
    acc[...] = bin_pieces(sup, split_pieces(square, pieces))
    copies[4].wait()
    frac[...] = fraction(sat[...])
    copies[5].wait()
    rate[...] = DT / pore[...]


def narrow_kernel(
    gathered, odd, p, perm, bs, p_middle, perm_middle, bs_middle, sat, small, acc_middle, out_odd, out_even, small_out, square
):
    even = lax.axis_index("narrow") % 2 == 0
    wide_even = lax.axis_index("wide") % 2 == 0
    mate = jnp.where(even, 1, 0)
    lanes = iota((NY, L), 1)

    def before(lo, n):
        return jnp.where(even, odd[lo : lo + n, :], gathered[mate, lo : lo + n, :])

    def after(lo, n):
        return jnp.where(even, gathered[mate, lo : lo + n, :], odd[lo : lo + n, :])

    in_slot = iota((8, L), 1) < 40

    def windows(get):
        out = []
        for i in range(5):
            block = get(N_SMALL + 8 * i, 8)
            out += [jnp.where(in_slot, roll(block, -40 * j, 1), 0.0) for j in range(3)]
        return out

    top, bottom = windows(before), windows(after)
    none = jnp.zeros((8, L), jnp.float32)
    stack = []
    for i in range(SMALL):
        own = small[i * TALL : (i + 1) * TALL, :]
        if i < ACC:
            own = own[8:24, :]
            stack.append(jnp.concatenate([top[i], own, bottom[i]], axis=0))
        else:
            stack.append(own + jnp.concatenate([top[i], top[i + 1], bottom[i + 1], bottom[i]], axis=0))
    pieces = jnp.zeros((NY, L), jnp.float32)
    for x, other_x, get in ((0, -1, before), (NX - 1, NX, after)):
        at = x * NY
        flux = trans_of(perm[0, at : at + NY, :], get(N_K, NY)) * (p[at : at + NY, :] - get(N_P, NY))
        for k in range(K):
            mine = lane_sum(bs[k, at : at + NY, :] * -flux)
            pieces = jnp.where(lanes == k * TALL + TOP + x, mine, pieces)
            other = lane_sum(get(N_B + k * NY, NY) * flux)
            pieces = jnp.where(lanes == k * TALL + TOP + other_x, other, pieces)
    stack[ACC] = stack[ACC] + acc_middle[...] + bin_pieces(stack[:K], split_pieces(square, pieces))
    for i in range(SMALL):
        small_out[i * TALL : (i + 1) * TALL, :] = stack[i]
    slot = iota((TALL, L), 1) // 8
    first = jnp.zeros((TALL, L), jnp.float32)
    last = jnp.zeros((TALL, L), jnp.float32)
    for i in range(SMALL):
        first = jnp.where(slot == i, roll(stack[i], 8 * i, 1), first)
        last = jnp.where(slot == i, roll(stack[i], 8 * i - 32, 1), last)
    for out, takes_last in ((out_even, wide_even), (out_odd, jnp.logical_not(wide_even))):
        col = jnp.where(takes_last, NY - 1, 0)
        for f in range(FIELDS):
            base = W_FIELD + f * COLUMN
            lo = N_C + f * 2 * EDGE
            out[base : base + EDGE, :] = jnp.where(takes_last, before(lo + EDGE, EDGE), before(lo, EDGE))
            base += EDGE
            for middle, x, n in ((False, 0, LOW), (True, LOW, HIGH - LOW), (False, HIGH, NX - HIGH)):
                rows = pl.ds((x - LOW) * NY + col if middle else x * NY + col, n, stride=NY)
                after_first = pl.ds((x - LOW + 1) * NY + col if middle else x * NY + col, n, stride=NY)
                if f == 0:
                    column = (p_middle if middle else p)[after_first, :]
                elif f == 1:
                    column = (perm_middle if middle else perm)[1, after_first, :]
                else:
                    column = (bs_middle if middle else bs)[f - 2, rows, :]
                out[base + x : base + x + n, :] = column
            base += NX
            out[base : base + EDGE, :] = jnp.where(takes_last, after(lo + EDGE, EDGE), after(lo, EDGE))
        out[W_SAT : W_SAT + NX, :] = sat[pl.ds(col, NX, stride=NY), :]
        out[W_SMALL : W_SMALL + COLUMN, :] = jnp.where(takes_last, last, first)[MARGIN : MARGIN + COLUMN, :]
        out[W_SMALL + COLUMN : W_ROWS, :] = jnp.zeros((W_ROWS - W_SMALL - COLUMN, L), jnp.float32)


def final_kernel(
    in_odd, in_even, sent_odd, sent_even, gathered, odd, small, p, perm, basis, trans,
    p_middle, basis_middle, trans_middle, sat, frac, rate,
    new_out, new_sat_out,
    new, new_sat, square, sems,
):
    even = lax.axis_index("narrow") % 2 == 0
    wide_even = lax.axis_index("wide") % 2 == 0
    mate = jnp.where(even, 1, 0)

    def before(lo, n):
        return jnp.where(even, odd[lo : lo + n, :], gathered[mate, lo : lo + n, :])

    def after(lo, n):
        return jnp.where(even, gathered[mate, lo : lo + n, :], odd[lo : lo + n, :])

    wide_mate = jnp.where(wide_even, 1, 0)

    def left(lo, n):
        return jnp.where(wide_even, in_odd[lo : lo + n, :], in_even[wide_mate, lo : lo + n, :])

    def right(lo, n):
        return jnp.where(wide_even, in_even[wide_mate, lo : lo + n, :], in_odd[lo : lo + n, :])

    def first(lo, n):
        return jnp.where(wide_even, sent_odd[lo : lo + n, :], sent_even[lo : lo + n, :])

    def last(lo, n):
        return jnp.where(wide_even, sent_even[lo : lo + n, :], sent_odd[lo : lo + n, :])

    lane = iota((TALL, L), 1)
    row = iota((TALL, L), 0)
    sent = jnp.logical_and(row >= MARGIN, row < MARGIN + COLUMN)

    def column_of(get, f):
        return get(W_FIELD + f * COLUMN - MARGIN, TALL)

    def own_rows(get, f):
        return get(W_FIELD + f * COLUMN + EDGE, NX)

    from_left, from_right = (jnp.where(sent, column_of(get, FIELDS), 0.0) for get in (left, right))
    stack = []
    for i in range(SMALL):
        own = small[i * TALL : (i + 1) * TALL, :]
        own = own + jnp.where(lane < 8, roll(from_left, -8 * i, 1), 0.0)
        own = own + jnp.where(lane // 8 == 4, roll(from_right, 32 - 8 * i, 1), 0.0)
        stack.append(own)
    sup, mat = stack[:K], stack[MAT : MAT + 9]
    pieces = [jnp.zeros((TALL, L), jnp.float32)] * K
    for mine, other, y, other_y in ((first, left, 0, -1), (last, right, NY - 1, NY)):
        k_here, k_there = column_of(mine, 1), column_of(other, 1)
        total = k_here + k_there
        flux = (2.0 * k_here * k_there / jnp.where(total > 0, total, 1.0)) * (
            column_of(mine, 0) - column_of(other, 0)
        )
        for k in range(K):
            here = lane_sum(column_of(mine, 2 + k) * -flux)
            there = lane_sum(column_of(other, 2 + k) * flux)
            pieces[k] = jnp.where(lane == WEST + y, here, pieces[k])
            pieces[k] = jnp.where(lane == WEST + other_y, there, pieces[k])
    res = stack[ACC] + bin_pieces(sup, pieces)
    diag = mat[4]
    scale = jnp.where(diag > 0, OMEGA / jnp.where(diag > 0, diag, 1.0), 0.0)

    def moved(coarse):
        sides = {dy: roll(coarse, -dy, 1) for dy in (-1, 0, 1)}
        return [roll(sides[dy], -dx, 0) for dx, dy in OFFSETS]

    coarse = scale * res
    for _ in range(SWEEPS - 1):
        rest = res
        for o, value in enumerate(moved(coarse)):
            rest = rest - mat[o] * value
        coarse = coarse + scale * rest
    shifts = moved(coarse)
    picked = []
    for k in range(K):
        total = jnp.zeros((TALL, L), jnp.float32)
        for o in range(9):
            total = jnp.where(sup[k] == float(o), shifts[o], total)
        picked.append(total)
    spread = jnp.zeros((TALL, L), jnp.float32)
    for k in range(K):
        spread = jnp.where(lane // NY == k, roll(picked[k], k * NY - WEST, 1), spread)
    spread = jnp.concatenate(halves(spread), axis=0)
    source = iota((L, L), 0)
    reorder = iota((L, L), 1) == (source % NY) * K + source // NY
    square[0 : 2 * TALL, :] = jnp.dot(
        spread, reorder.astype(jnp.bfloat16), preferred_element_type=jnp.float32
    )
    square[2 * TALL :, :] = spread.astype(jnp.float32)
    rows, lanes = iota((NY, L), 0), iota((NY, L), 1)

    def prolonged(values, start, x, mine):
        parts = []
        for at in (start, start + TALL):
            parts.append(jnp.where(mine, square[at + TOP + x : at + TOP + x + 1, :], 0.0))
        weights = jnp.concatenate(parts, axis=0).astype(jnp.bfloat16)
        both = jnp.dot(weights, values, preferred_element_type=jnp.float32)
        return both[:NY, :] + both[NY:, :]

    own = lanes // K == rows
    for x in range(NX):
        at = slice(x * NY, (x + 1) * NY)
        inner = LOW <= x < HIGH
        before_x = p_middle[(x - LOW + 1) * NY : (x - LOW + 2) * NY, :] if inner else p[at, :]
        ref, base = (basis_middle, LOW) if inner else (basis, 0)
        values = ref[(x - base) * NY * K : (x - base + 1) * NY * K, :]
        new[at, :] = before_x + prolonged(values, 0, x, own)
    copies = copies_of(sems, [(new, new_out)])
    ends = []
    own = lanes % NY == rows
    for get, x in ((before, -1), (after, NX)):
        values = get(N_B, K * NY).astype(jnp.bfloat16)
        ends.append(get(N_P, NY) + prolonged(values, 2 * TALL, x, own))
    sides = []
    for get, y in ((left, -1), (right, NY)):
        total = own_rows(get, 0)
        for k in range(K):
            column = picked[k][TOP : TOP + NX, WEST + y : WEST + y + 1]
            total = total + own_rows(get, 2 + k) * column
        sides.append(total)

    def carried(value, here, there, f_here, f_there):
        flux = value * (here - there)
        return flux * jnp.where(flux > 0, f_here, f_there)

    west_f, east_f = fraction(left(W_SAT, NX)), fraction(right(W_SAT, NX))
    east_t = trans_of(own_rows(last, 1), own_rows(right, 1))
    west_flow = carried(
        trans_of(own_rows(first, 1), own_rows(left, 1)),
        sides[0],
        new[pl.ds(0, NX, stride=NY), :],
        west_f,
        frac[pl.ds(0, NX, stride=NY), :],
    )
    end = rows == NY - 1
    done = 0
    p_here, f_here = new[0:NY, :], frac[0:NY, :]
    flow_in = carried(
        trans_of(before(N_K, NY), perm[0, 0:NY, :]), ends[0], p_here, fraction(before(N_S, NY)), f_here
    )
    for x in range(NX):
        at = slice(x * NY, (x + 1) * NY)
        ref, base = (trans_middle, LOW - 1) if LOW <= x < HIGH else (trans, 0)
        tx, ty, tz = (ref[c, (x - base) * NY : (x - base + 1) * NY, :] for c in range(3))
        if x < NX - 1:
            nxt = slice((x + 1) * NY, (x + 2) * NY)
            p_next, f_next = new[nxt, :], frac[nxt, :]
        else:
            p_next, f_next = ends[1], fraction(after(N_S, NY))
            tx = trans_of(perm[0, at, :], after(N_K, NY))
        flow_out = carried(tx, p_here, p_next, f_here, f_next)
        total = flow_out - flow_in
        flow_in = flow_out
        beside = lambda a, e: jnp.where(end, e[x : x + 1, :], roll(a, -1, 0))
        fy = carried(
            jnp.where(end, east_t[x : x + 1, :], ty),
            p_here,
            beside(p_here, sides[1]),
            f_here,
            beside(f_here, east_f),
        )
        total = total + (fy - jnp.where(rows == 0, west_flow[x : x + 1, :], roll(fy, 1, 0)))
        fz = carried(tz, p_here, roll(p_here, -1, 1), f_here, roll(f_here, -1, 1))
        total = total + (fz - roll(fz, 1, 1))
        new_sat[at, :] = sat[at, :] - rate[at, :] * total
        p_here, f_here = p_next, f_next
        if x in CHUNKS:
            part = pl.ds(done * NY, (x + 1 - done) * NY)
            copy = pltpu.make_async_copy(new_sat.at[part], new_sat_out.at[part], sems.at[len(copies)])
            copy.start()
            copies.append(copy)
            done = x + 1
    for copy in copies:
        copy.wait()


VMEM = pl.BlockSpec(memory_space=pltpu.VMEM)
HBM = pl.BlockSpec(memory_space=pltpu.HBM)


def call(kernel, outs, scratch, flops, args, far=0, out_spec=VMEM):
    args = [pltpu.with_memory_space_constraint(a, pltpu.HBM) for a in args[:far]] + args[far:]
    shapes = [jax.ShapeDtypeStruct(o[:-1], o[-1]) if isinstance(o[-1], type) else jax.ShapeDtypeStruct(o, jnp.float32) for o in outs]
    size = sum(a.size * a.dtype.itemsize for a in [*args, *shapes])
    return pl.pallas_call(
        kernel,
        out_shape=shapes,
        in_specs=[HBM] * far + [VMEM] * (len(args) - far),
        out_specs=[out_spec] * len(shapes),
        scratch_shapes=scratch,
        compiler_params=pltpu.CompilerParams(vmem_limit_bytes=24 * 1024 * 1024),
        cost_estimate=pl.CostEstimate(flops=flops, bytes_accessed=size, transcendentals=0),
    )(*args)


def space(*shape, dtype=jnp.float32):
    return pltpu.VMEM(shape, dtype)


def swaps(n, start):
    pairs = [(i, i + 1) for i in range(start, n - 1, 2)]
    return pairs + [(j, i) for i, j in pairs]


def on_device(pressure, saturation, source, permeability, pore_volume, basis, support, matrix):
    p_in, sat_in, src_in, pore_in = (
        a.reshape(-1, L) for a in (pressure, saturation, source, pore_volume)
    )
    perm_in = permeability.reshape(3, -1, L)
    basis_in = basis.reshape(-1, L)
    support = support.transpose(0, 2, 1).reshape(NX * K, NY)
    matrix = matrix.reshape(9 * NX, NY)
    n_narrow, n_wide = lax.axis_size("narrow"), lax.axis_size("wide")
    cells, fine, middle = NX * NY, NX * NY * K, (HIGH - LOW) * NY
    near = middle + 2 * NY
    out_even, out_odd, small, p, perm, bs, trans, basis = call(
        edge_kernel,
        [(N_ROWS, L), (N_ROWS, L), (SMALL * TALL, L), (cells, L), (3, cells, L), (K, cells, L), (3, cells, L),
         (fine, L, jnp.bfloat16)],
        [
            space(cells, L), space(fine, L), space(NX * K, NY, dtype=jnp.int32),
            space(9 * NX, NY), space(TALL, L), space(L, L), pltpu.SemaphoreType.DMA((12,)),
        ],
        10**7,
        [p_in, perm_in, src_in, basis_in, support, matrix, sat_in],
        far=7,
    )
    odd = lax.ppermute(out_odd, "narrow", swaps(n_narrow, 1))
    gathered = lax.all_gather(
        out_even, "narrow", axis_index_groups=[[i, i + 1] for i in range(0, n_narrow, 2)]
    )
    p_middle, perm_middle, bs_middle, trans_middle, acc, sat, frac, rate, basis_middle = call(
        middle_kernel,
        [
            (near, L), (3, near, L), (K, middle, L), (3, near, L), (TALL, L), (cells, L), (cells, L), (cells, L),
            (middle * K, L, jnp.bfloat16),
        ],
        [
            space(near, L), space(middle * K, L), space(cells, L),
            space(L, L), pltpu.SemaphoreType.DMA((6,)),
        ],
        10**7,
        [p_in, perm_in, src_in, basis_in, sat_in, pore_in, small],
        far=6,
    )
    sent_odd, sent_even, small = call(
        narrow_kernel,
        [(W_ROWS, L), (W_ROWS, L), (SMALL * TALL, L)],
        [space(L, L)],
        10**6,
        [gathered, odd, p, perm, bs, p_middle, perm_middle, bs_middle, sat, small, acc],
    )
    in_odd = lax.ppermute(sent_odd, "wide", swaps(n_wide, 1))
    in_even = lax.all_gather(
        sent_even, "wide", axis_index_groups=[[i, i + 1] for i in range(0, n_wide, 2)]
    )
    new, new_sat = call(
        final_kernel,
        [(cells, L), (cells, L)],
        [space(cells, L), space(cells, L), space(L, L), pltpu.SemaphoreType.DMA((5,))],
        10**7,
        [
            in_odd, in_even, sent_odd, sent_even, gathered, odd, small, p, perm, basis, trans,
            p_middle, basis_middle, trans_middle, sat, frac, rate,
        ],
        out_spec=HBM,
    )
    return new.reshape(pressure.shape), new_sat.reshape(pressure.shape)


def solution(mesh):
    return jax.shard_map(
        on_device,
        mesh=mesh,
        in_specs=(
            P("narrow", "wide", None),
            P("narrow", "wide", None),
            P("narrow", "wide", None),
            P(None, "narrow", "wide", None),
            P("narrow", "wide", None),
            P("narrow", "wide", None, None),
            P("narrow", "wide", None),
            P(None, "narrow", "wide"),
        ),
        out_specs=(P("narrow", "wide", None), P("narrow", "wide", None)),
        check_vma=False,
    )
```

```python
import jax
import jax.numpy as jnp
from jax import lax
from jax.experimental import pallas as pl
from jax.experimental.pallas import tpu as pltpu
from jax.sharding import PartitionSpec as P

SWEEPS = 3
OFFSETS = [(o // 3 - 1, o % 3 - 1) for o in range(9)]
OMEGA = 0.6667
DT = 0.01

NX, NY, L, K = 16, 32, 128, 4
TOP, WEST, TALL = 8, 4, 32
EDGE = 5
FIELDS = 2 + K
SUP, MAT, ACC = 0, K, K + 9
SMALL = K + 10
N_P, N_K, N_S, N_B, N_C = 0, 32, 64, 96, 224
N_SMALL = 288
N_ROWS = N_SMALL + 8 * 5
COLUMN = NX + 2 * EDGE
MARGIN = TOP - EDGE
W_SAT = 0
W_FIELD = NX
W_SMALL = W_FIELD + FIELDS * COLUMN
W_ROWS = W_SMALL + COLUMN + 10


def roll(a, shift, axis):
    shift %= a.shape[axis]
    return pltpu.roll(a, shift, axis) if shift else a


def iota(shape, axis):
    return lax.broadcasted_iota(jnp.int32, shape, axis)


def trans_of(here, there):
    return 2.0 * here * there / (here + there)


def fraction(sat):
    rest = 1.0 - sat
    square = sat * sat
    return square / (square + 0.5 * (rest * rest))


def lane_sum(a):
    return jnp.sum(a, axis=-1, keepdims=True)


def halves(a):
    high = a.astype(jnp.bfloat16)
    return high, (a - high.astype(jnp.float32)).astype(jnp.bfloat16)


def bin_pieces(sup, pieces):
    total = None
    for dy in (-1, 0, 1):
        column = None
        for dx in (-1, 0, 1):
            code = float((dx + 1) * 3 + dy + 1)
            part = None
            for k in range(K):
                term = jnp.where(sup[k] == code, pieces[k], 0.0)
                part = term if part is None else part + term
            part = roll(part, dx, 0)
            column = part if column is None else column + part
        column = roll(column, dy, 1)
        total = column if total is None else total + column
    return total


def turned(scratch, value):
    scratch[...] = jnp.zeros((L, L), jnp.float32)
    scratch[WEST : WEST + NY, :] = value
    return scratch[...].T


def rows_residual(p, perm, src, trans, lo, hi, base):
    rows, lanes = iota((NY, L), 0), iota((NY, L), 1)

    def face(x):
        a, b = slice((x - base) * NY, (x - base + 1) * NY), slice((x - base + 1) * NY, (x - base + 2) * NY)
        value = trans_of(perm[0, a, :], perm[0, b, :])
        trans[0, a, :] = value
        return value * (p[a, :] - p[b, :])

    result = []
    last = face(lo - 1) if lo > 0 else None
    for x in range(lo, hi):
        at = slice((x - base) * NY, (x - base + 1) * NY)
        here, ky, kz = p[at, :], perm[1, at, :], perm[2, at, :]
        ty = jnp.where(rows < NY - 1, trans_of(ky, roll(ky, -1, 0)), 0.0)
        tz = jnp.where(lanes < L - 1, trans_of(kz, roll(kz, -1, 1)), 0.0)
        trans[1, at, :] = ty
        trans[2, at, :] = tz
        fy = ty * (here - roll(here, -1, 0))
        fz = tz * (here - roll(here, -1, 1))
        total = (fy - roll(fy, 1, 0)) + (fz - roll(fz, 1, 1))
        if last is not None:
            total = total - last
        last = None
        if x < NX - 1:
            last = face(x)
            total = total + last
        result.append(src[at, :] - total)
    return result


def add_pieces(pieces, residuals, lo, mixed, bs, base):
    lanes = iota((NY, L), 1)
    for i, res in enumerate(residuals):
        x = lo + i
        for k in range(K):
            b = mixed[pl.ds((x - base) * NY * K + k, NY, stride=K), :]
            bs[k, (x - base) * NY : (x - base + 1) * NY, :] = b
            pieces = jnp.where(lanes == k * TALL + TOP + x, lane_sum(b * res), pieces)
    return pieces


def split_pieces(square, pieces):
    flipped = turned(square, pieces)
    return [flipped[k * TALL : (k + 1) * TALL, :] for k in range(K)]


CHUNKS = (4, 9, 13, NX - 1)
LOW, HIGH = EDGE, NX - EDGE


def copies_of(sems, pairs):
    out = [pltpu.make_async_copy(src, dst, sems.at[i]) for i, (src, dst) in enumerate(pairs)]
    for copy in out:
        copy.start()
    return out


def edge_kernel(
    p_in, perm_in, src_in, basis_in, support_in, matrix_in, sat_in,
    out_even, out_odd, small, p, perm, bs, trans, basis,
    src, mixed, support, matrix, place, square, sems,
):
    even = lax.axis_index("narrow") % 2 == 0
    rows_even = pl.ds(pl.multiple_of(jnp.where(even, NX - 1, 0) * NY, NY), NY)
    rows_odd = pl.ds(pl.multiple_of(jnp.where(even, 0, NX - 1) * NY, NY), NY)
    pairs = [(support_in, support), (matrix_in, matrix)]
    for near, first in ((0, 0), (HIGH - 1, HIGH)):
        part = pl.ds(near * NY, (EDGE + 1) * NY)
        own, fine = pl.ds(first * NY, EDGE * NY), pl.ds(first * NY * K, EDGE * NY * K)
        pairs += [(p_in.at[part], p.at[part]), (perm_in.at[:, part], perm.at[:, part])]
        pairs += [(src_in.at[own], src.at[own]), (basis_in.at[fine], basis.at[fine])]
    pairs += [(sat_in.at[rows_even], out_even.at[pl.ds(N_S, NY)])]
    pairs += [(sat_in.at[rows_odd], out_odd.at[pl.ds(N_S, NY)])]
    copies = copies_of(sems, pairs)
    copies[0].wait()
    copies[1].wait()
    place[...] = jnp.zeros((TALL, L), jnp.float32)
    for i in range(K + 9):
        if i < MAT:
            value = support[pl.ds(i, NX, stride=K), :].astype(jnp.float32)
        else:
            value = matrix[(i - MAT) * NX : (i - MAT + 1) * NX, :]
        place[TOP : TOP + NX, 0:NY] = value
        small[i * TALL : (i + 1) * TALL, :] = roll(place[...], WEST, 1)
    pieces = jnp.zeros((NY, L), jnp.float32)
    for i, first in enumerate((0, HIGH)):
        for copy in copies[4 * i + 2 : 4 * i + 5]:
            copy.wait()
        residuals = rows_residual(p, perm, src, trans, first, first + EDGE, 0)
        copies[4 * i + 5].wait()
        fine = slice(first * NY * K, (first + EDGE) * NY * K)
        mixed[fine, :] = basis[fine, :].astype(jnp.float32)
        pieces = add_pieces(pieces, residuals, first, mixed, bs, 0)
    pieces = split_pieces(square, pieces)
    stack = [small[i * TALL : (i + 1) * TALL, :] for i in range(ACC)]
    acc = bin_pieces(stack[:K], pieces)
    stack.append(acc)
    small[ACC * TALL : SMALL * TALL, :] = acc
    for out, takes_last in ((out_even, even), (out_odd, jnp.logical_not(even))):
        edge = jnp.where(takes_last, NX - 1, 0)
        row = pl.multiple_of(edge * NY, NY)
        out[N_P : N_P + NY, :] = p[pl.ds(row, NY), :]
        out[N_K : N_K + NY, :] = perm[0, pl.ds(row, NY), :]
        for k in range(K):
            out[N_B + k * NY : N_B + (k + 1) * NY, :] = bs[k, pl.ds(row, NY), :]
        start = jnp.where(takes_last, NX - EDGE, 0) * NY
        for c, col in enumerate((0, NY - 1)):
            fields = [
                p[pl.ds(start + col, EDGE, stride=NY), :],
                perm[1, pl.ds(start + col, EDGE, stride=NY), :],
            ] + [bs[k, pl.ds(start + col, EDGE, stride=NY), :] for k in range(K)]
            for f, value in enumerate(fields):
                to = N_C + (f * 2 + c) * EDGE
                out[to : to + EDGE, :] = value
        window = [jnp.where(takes_last, s[16:24, :], s[8:16, :]) for s in stack]
        window.append(jnp.where(takes_last, acc[24:32, :], acc[0:8, :]))
        for i in range(5):
            a, b, c = window[3 * i : 3 * i + 3]
            out[N_SMALL + 8 * i : N_SMALL + 8 * i + 8, :] = a + roll(b, 40, 1) + roll(c, 80, 1)
    copies[10].wait()
    copies[11].wait()


def middle_kernel(
    p_in, perm_in, src_in, basis_in, sat_in, pore_in, small,
    p, perm, bs, trans, acc, sat, frac, rate, basis,
    src, mixed, pore, square, sems,
):
    near = pl.ds((LOW - 1) * NY, (HIGH - LOW + 2) * NY)
    own, fine = pl.ds(LOW * NY, (HIGH - LOW) * NY), pl.ds(LOW * NY * K, (HIGH - LOW) * NY * K)
    inner = pl.ds(NY, (HIGH - LOW) * NY)
    copies = copies_of(
        sems,
        [
            (sat_in, sat), (pore_in, pore), (p_in.at[near], p), (perm_in.at[:, near], perm),
            (src_in.at[own], src.at[inner]), (basis_in.at[fine], basis),
        ],
    )
    copies[0].wait()
    frac[...] = fraction(sat[...])
    copies[1].wait()
    rate[...] = DT / pore[...]
    for copy in copies[2:5]:
        copy.wait()
    residuals = rows_residual(p, perm, src, trans, LOW, HIGH, LOW - 1)
    copies[5].wait()
    mixed[...] = basis[...].astype(jnp.float32)
    pieces = add_pieces(jnp.zeros((NY, L), jnp.float32), residuals, LOW, mixed, bs, LOW)
    sup = [small[k * TALL : (k + 1) * TALL, :] for k in range(K)]
    acc[...] = bin_pieces(sup, split_pieces(square, pieces))


def narrow_kernel(
    gathered, odd, p, perm, bs, p_middle, perm_middle, bs_middle, sat, small, acc_middle, out_odd, out_even, small_out, square
):
    even = lax.axis_index("narrow") % 2 == 0
    wide_even = lax.axis_index("wide") % 2 == 0
    mate = jnp.where(even, 1, 0)
    lanes = iota((NY, L), 1)

    def before(lo, n):
        return jnp.where(even, odd[lo : lo + n, :], gathered[mate, lo : lo + n, :])

    def after(lo, n):
        return jnp.where(even, gathered[mate, lo : lo + n, :], odd[lo : lo + n, :])

    in_slot = iota((8, L), 1) < 40

    def windows(get):
        out = []
        for i in range(5):
            block = get(N_SMALL + 8 * i, 8)
            out += [jnp.where(in_slot, roll(block, -40 * j, 1), 0.0) for j in range(3)]
        return out

    top, bottom = windows(before), windows(after)
    none = jnp.zeros((8, L), jnp.float32)
    stack = []
    for i in range(SMALL):
        own = small[i * TALL : (i + 1) * TALL, :]
        if i < ACC:
            own = own[8:24, :]
            stack.append(jnp.concatenate([top[i], own, bottom[i]], axis=0))
        else:
            stack.append(own + jnp.concatenate([top[i], top[i + 1], bottom[i + 1], bottom[i]], axis=0))
    pieces = jnp.zeros((NY, L), jnp.float32)
    for x, other_x, get in ((0, -1, before), (NX - 1, NX, after)):
        at = x * NY
        flux = trans_of(perm[0, at : at + NY, :], get(N_K, NY)) * (p[at : at + NY, :] - get(N_P, NY))
        for k in range(K):
            mine = lane_sum(bs[k, at : at + NY, :] * -flux)
            pieces = jnp.where(lanes == k * TALL + TOP + x, mine, pieces)
            other = lane_sum(get(N_B + k * NY, NY) * flux)
            pieces = jnp.where(lanes == k * TALL + TOP + other_x, other, pieces)
    stack[ACC] = stack[ACC] + acc_middle[...] + bin_pieces(stack[:K], split_pieces(square, pieces))
    for i in range(SMALL):
        small_out[i * TALL : (i + 1) * TALL, :] = stack[i]
    slot = iota((TALL, L), 1) // 8
    first = jnp.zeros((TALL, L), jnp.float32)
    last = jnp.zeros((TALL, L), jnp.float32)
    for i in range(SMALL):
        first = jnp.where(slot == i, roll(stack[i], 8 * i, 1), first)
        last = jnp.where(slot == i, roll(stack[i], 8 * i - 32, 1), last)
    for out, takes_last in ((out_even, wide_even), (out_odd, jnp.logical_not(wide_even))):
        col = jnp.where(takes_last, NY - 1, 0)
        for f in range(FIELDS):
            base = W_FIELD + f * COLUMN
            lo = N_C + f * 2 * EDGE
            out[base : base + EDGE, :] = jnp.where(takes_last, before(lo + EDGE, EDGE), before(lo, EDGE))
            base += EDGE
            for middle, x, n in ((False, 0, LOW), (True, LOW, HIGH - LOW), (False, HIGH, NX - HIGH)):
                rows = pl.ds((x - LOW) * NY + col if middle else x * NY + col, n, stride=NY)
                after_first = pl.ds((x - LOW + 1) * NY + col if middle else x * NY + col, n, stride=NY)
                if f == 0:
                    column = (p_middle if middle else p)[after_first, :]
                elif f == 1:
                    column = (perm_middle if middle else perm)[1, after_first, :]
                else:
                    column = (bs_middle if middle else bs)[f - 2, rows, :]
                out[base + x : base + x + n, :] = column
            base += NX
            out[base : base + EDGE, :] = jnp.where(takes_last, after(lo + EDGE, EDGE), after(lo, EDGE))
        out[W_SAT : W_SAT + NX, :] = sat[pl.ds(col, NX, stride=NY), :]
        out[W_SMALL : W_SMALL + COLUMN, :] = jnp.where(takes_last, last, first)[MARGIN : MARGIN + COLUMN, :]
        out[W_SMALL + COLUMN : W_ROWS, :] = jnp.zeros((W_ROWS - W_SMALL - COLUMN, L), jnp.float32)


def final_kernel(
    in_odd, in_even, sent_odd, sent_even, gathered, odd, small, p, perm, basis, trans,
    p_middle, basis_middle, trans_middle, sat, frac, rate,
    new_out, new_sat_out,
    new, new_sat, square, sems,
):
    even = lax.axis_index("narrow") % 2 == 0
    wide_even = lax.axis_index("wide") % 2 == 0
    mate = jnp.where(even, 1, 0)

    def before(lo, n):
        return jnp.where(even, odd[lo : lo + n, :], gathered[mate, lo : lo + n, :])

    def after(lo, n):
        return jnp.where(even, gathered[mate, lo : lo + n, :], odd[lo : lo + n, :])

    wide_mate = jnp.where(wide_even, 1, 0)

    def left(lo, n):
        return jnp.where(wide_even, in_odd[lo : lo + n, :], in_even[wide_mate, lo : lo + n, :])

    def right(lo, n):
        return jnp.where(wide_even, in_even[wide_mate, lo : lo + n, :], in_odd[lo : lo + n, :])

    def first(lo, n):
        return jnp.where(wide_even, sent_odd[lo : lo + n, :], sent_even[lo : lo + n, :])

    def last(lo, n):
        return jnp.where(wide_even, sent_even[lo : lo + n, :], sent_odd[lo : lo + n, :])

    lane = iota((TALL, L), 1)
    row = iota((TALL, L), 0)
    sent = jnp.logical_and(row >= MARGIN, row < MARGIN + COLUMN)

    def column_of(get, f):
        return get(W_FIELD + f * COLUMN - MARGIN, TALL)

    def own_rows(get, f):
        return get(W_FIELD + f * COLUMN + EDGE, NX)

    from_left, from_right = (jnp.where(sent, column_of(get, FIELDS), 0.0) for get in (left, right))
    stack = []
    for i in range(SMALL):
        own = small[i * TALL : (i + 1) * TALL, :]
        own = own + jnp.where(lane < 8, roll(from_left, -8 * i, 1), 0.0)
        own = own + jnp.where(lane // 8 == 4, roll(from_right, 32 - 8 * i, 1), 0.0)
        stack.append(own)
    sup, mat = stack[:K], stack[MAT : MAT + 9]
    pieces = [jnp.zeros((TALL, L), jnp.float32)] * K
    for mine, other, y, other_y in ((first, left, 0, -1), (last, right, NY - 1, NY)):
        k_here, k_there = column_of(mine, 1), column_of(other, 1)
        total = k_here + k_there
        flux = (2.0 * k_here * k_there / jnp.where(total > 0, total, 1.0)) * (
            column_of(mine, 0) - column_of(other, 0)
        )
        for k in range(K):
            here = lane_sum(column_of(mine, 2 + k) * -flux)
            there = lane_sum(column_of(other, 2 + k) * flux)
            pieces[k] = jnp.where(lane == WEST + y, here, pieces[k])
            pieces[k] = jnp.where(lane == WEST + other_y, there, pieces[k])
    res = stack[ACC] + bin_pieces(sup, pieces)
    diag = mat[4]
    scale = jnp.where(diag > 0, OMEGA / jnp.where(diag > 0, diag, 1.0), 0.0)

    def moved(coarse):
        sides = {dy: roll(coarse, -dy, 1) for dy in (-1, 0, 1)}
        return [roll(sides[dy], -dx, 0) for dx, dy in OFFSETS]

    coarse = scale * res
    for _ in range(SWEEPS - 1):
        rest = res
        for o, value in enumerate(moved(coarse)):
            rest = rest - mat[o] * value
        coarse = coarse + scale * rest
    shifts = moved(coarse)
    picked = []
    for k in range(K):
        total = jnp.zeros((TALL, L), jnp.float32)
        for o in range(9):
            total = jnp.where(sup[k] == float(o), shifts[o], total)
        picked.append(total)
    spread = jnp.zeros((TALL, L), jnp.float32)
    for k in range(K):
        spread = jnp.where(lane // NY == k, roll(picked[k], k * NY - WEST, 1), spread)
    spread = jnp.concatenate(halves(spread), axis=0)
    source = iota((L, L), 0)
    reorder = iota((L, L), 1) == (source % NY) * K + source // NY
    square[0 : 2 * TALL, :] = jnp.dot(
        spread, reorder.astype(jnp.bfloat16), preferred_element_type=jnp.float32
    )
    square[2 * TALL :, :] = spread.astype(jnp.float32)
    rows, lanes = iota((NY, L), 0), iota((NY, L), 1)

    def prolonged(values, start, x, mine):
        parts = []
        for at in (start, start + TALL):
            parts.append(jnp.where(mine, square[at + TOP + x : at + TOP + x + 1, :], 0.0))
        weights = jnp.concatenate(parts, axis=0).astype(jnp.bfloat16)
        both = jnp.dot(weights, values, preferred_element_type=jnp.float32)
        return both[:NY, :] + both[NY:, :]

    own = lanes // K == rows
    for x in range(NX):
        at = slice(x * NY, (x + 1) * NY)
        inner = LOW <= x < HIGH
        before_x = p_middle[(x - LOW + 1) * NY : (x - LOW + 2) * NY, :] if inner else p[at, :]
        ref, base = (basis_middle, LOW) if inner else (basis, 0)
        values = ref[(x - base) * NY * K : (x - base + 1) * NY * K, :]
        new[at, :] = before_x + prolonged(values, 0, x, own)
    copies = copies_of(sems, [(new, new_out)])
    ends = []
    own = lanes % NY == rows
    for get, x in ((before, -1), (after, NX)):
        values = get(N_B, K * NY).astype(jnp.bfloat16)
        ends.append(get(N_P, NY) + prolonged(values, 2 * TALL, x, own))
    sides = []
    for get, y in ((left, -1), (right, NY)):
        total = own_rows(get, 0)
        for k in range(K):
            column = picked[k][TOP : TOP + NX, WEST + y : WEST + y + 1]
            total = total + own_rows(get, 2 + k) * column
        sides.append(total)

    def carried(value, here, there, f_here, f_there):
        flux = value * (here - there)
        return flux * jnp.where(flux > 0, f_here, f_there)

    west_f, east_f = fraction(left(W_SAT, NX)), fraction(right(W_SAT, NX))
    east_t = trans_of(own_rows(last, 1), own_rows(right, 1))
    west_flow = carried(
        trans_of(own_rows(first, 1), own_rows(left, 1)),
        sides[0],
        new[pl.ds(0, NX, stride=NY), :],
        west_f,
        frac[pl.ds(0, NX, stride=NY), :],
    )
    end = rows == NY - 1
    done = 0
    p_here, f_here = new[0:NY, :], frac[0:NY, :]
    flow_in = carried(
        trans_of(before(N_K, NY), perm[0, 0:NY, :]), ends[0], p_here, fraction(before(N_S, NY)), f_here
    )
    for x in range(NX):
        at = slice(x * NY, (x + 1) * NY)
        ref, base = (trans_middle, LOW - 1) if LOW <= x < HIGH else (trans, 0)
        tx, ty, tz = (ref[c, (x - base) * NY : (x - base + 1) * NY, :] for c in range(3))
        if x < NX - 1:
            nxt = slice((x + 1) * NY, (x + 2) * NY)
            p_next, f_next = new[nxt, :], frac[nxt, :]
        else:
            p_next, f_next = ends[1], fraction(after(N_S, NY))
            tx = trans_of(perm[0, at, :], after(N_K, NY))
        flow_out = carried(tx, p_here, p_next, f_here, f_next)
        total = flow_out - flow_in
        flow_in = flow_out
        beside = lambda a, e: jnp.where(end, e[x : x + 1, :], roll(a, -1, 0))
        fy = carried(
            jnp.where(end, east_t[x : x + 1, :], ty),
            p_here,
            beside(p_here, sides[1]),
            f_here,
            beside(f_here, east_f),
        )
        total = total + (fy - jnp.where(rows == 0, west_flow[x : x + 1, :], roll(fy, 1, 0)))
        fz = carried(tz, p_here, roll(p_here, -1, 1), f_here, roll(f_here, -1, 1))
        total = total + (fz - roll(fz, 1, 1))
        new_sat[at, :] = sat[at, :] - rate[at, :] * total
        p_here, f_here = p_next, f_next
        if x in CHUNKS:
            part = pl.ds(done * NY, (x + 1 - done) * NY)
            copy = pltpu.make_async_copy(new_sat.at[part], new_sat_out.at[part], sems.at[len(copies)])
            copy.start()
            copies.append(copy)
            done = x + 1
    for copy in copies:
        copy.wait()


VMEM = pl.BlockSpec(memory_space=pltpu.VMEM)
HBM = pl.BlockSpec(memory_space=pltpu.HBM)


def call(kernel, outs, scratch, flops, args, far=0, out_spec=VMEM):
    args = [pltpu.with_memory_space_constraint(a, pltpu.HBM) for a in args[:far]] + args[far:]
    shapes = [jax.ShapeDtypeStruct(o[:-1], o[-1]) if isinstance(o[-1], type) else jax.ShapeDtypeStruct(o, jnp.float32) for o in outs]
    size = sum(a.size * a.dtype.itemsize for a in [*args, *shapes])
    return pl.pallas_call(
        kernel,
        out_shape=shapes,
        in_specs=[HBM] * far + [VMEM] * (len(args) - far),
        out_specs=[out_spec] * len(shapes),
        scratch_shapes=scratch,
        compiler_params=pltpu.CompilerParams(vmem_limit_bytes=24 * 1024 * 1024),
        cost_estimate=pl.CostEstimate(flops=flops, bytes_accessed=size, transcendentals=0),
    )(*args)


def space(*shape, dtype=jnp.float32):
    return pltpu.VMEM(shape, dtype)


def swaps(n, start):
    pairs = [(i, i + 1) for i in range(start, n - 1, 2)]
    return pairs + [(j, i) for i, j in pairs]


def on_device(pressure, saturation, source, permeability, pore_volume, basis, support, matrix):
    p_in, sat_in, src_in, pore_in = (
        a.reshape(-1, L) for a in (pressure, saturation, source, pore_volume)
    )
    perm_in = permeability.reshape(3, -1, L)
    basis_in = basis.reshape(-1, L)
    support = support.transpose(0, 2, 1).reshape(NX * K, NY)
    matrix = matrix.reshape(9 * NX, NY)
    n_narrow, n_wide = lax.axis_size("narrow"), lax.axis_size("wide")
    cells, fine, middle = NX * NY, NX * NY * K, (HIGH - LOW) * NY
    near = middle + 2 * NY
    out_even, out_odd, small, p, perm, bs, trans, basis = call(
        edge_kernel,
        [(N_ROWS, L), (N_ROWS, L), (SMALL * TALL, L), (cells, L), (3, cells, L), (K, cells, L), (3, cells, L),
         (fine, L, jnp.bfloat16)],
        [
            space(cells, L), space(fine, L), space(NX * K, NY, dtype=jnp.int32),
            space(9 * NX, NY), space(TALL, L), space(L, L), pltpu.SemaphoreType.DMA((12,)),
        ],
        10**7,
        [p_in, perm_in, src_in, basis_in, support, matrix, sat_in],
        far=7,
    )
    odd = lax.ppermute(out_odd, "narrow", swaps(n_narrow, 1))
    gathered = lax.all_gather(
        out_even, "narrow", axis_index_groups=[[i, i + 1] for i in range(0, n_narrow, 2)]
    )
    p_middle, perm_middle, bs_middle, trans_middle, acc, sat, frac, rate, basis_middle = call(
        middle_kernel,
        [
            (near, L), (3, near, L), (K, middle, L), (3, near, L), (TALL, L), (cells, L), (cells, L), (cells, L),
            (middle * K, L, jnp.bfloat16),
        ],
        [
            space(near, L), space(middle * K, L), space(cells, L),
            space(L, L), pltpu.SemaphoreType.DMA((6,)),
        ],
        10**7,
        [p_in, perm_in, src_in, basis_in, sat_in, pore_in, small],
        far=6,
    )
    sent_odd, sent_even, small = call(
        narrow_kernel,
        [(W_ROWS, L), (W_ROWS, L), (SMALL * TALL, L)],
        [space(L, L)],
        10**6,
        [gathered, odd, p, perm, bs, p_middle, perm_middle, bs_middle, sat, small, acc],
    )
    in_odd = lax.ppermute(sent_odd, "wide", swaps(n_wide, 1))
    in_even = lax.all_gather(
        sent_even, "wide", axis_index_groups=[[i, i + 1] for i in range(0, n_wide, 2)]
    )
    new, new_sat = call(
        final_kernel,
        [(cells, L), (cells, L)],
        [space(cells, L), space(cells, L), space(L, L), pltpu.SemaphoreType.DMA((5,))],
        10**7,
        [
            in_odd, in_even, sent_odd, sent_even, gathered, odd, small, p, perm, basis, trans,
            p_middle, basis_middle, trans_middle, sat, frac, rate,
        ],
        out_spec=HBM,
    )
    return new.reshape(pressure.shape), new_sat.reshape(pressure.shape)


def solution(mesh):
    return jax.shard_map(
        on_device,
        mesh=mesh,
        in_specs=(
            P("narrow", "wide", None),
            P("narrow", "wide", None),
            P("narrow", "wide", None),
            P(None, "narrow", "wide", None),
            P("narrow", "wide", None),
            P("narrow", "wide", None, None),
            P("narrow", "wide", None),
            P(None, "narrow", "wide"),
        ),
        out_specs=(P("narrow", "wide", None), P("narrow", "wide", None)),
        check_vma=False,
    )
```
